32 devices in a mesh: section: 2 (over x), expert: 16 (over z, y, core).
Axes of the slice: x: 2, y: 2, z: 4, core: 2. Of those that a mesh axis runs over, the one named last changes fastest.
Arguments:
- tokens: bfloat16 [384, 7168], P('expert', 'section'), may hold values from -6 to 6
- expert_ids: int32 [384, 8], P('expert'), may hold values from 0 to 15, all different within a row; in each aligned block of 24 rows (0 to 23, 24 to 47, ...) at most 16 rows name the same one
- gate_weights: bfloat16 [384, 8], P('expert'), may hold values from 0.099609375 to 0.59765625
- w_gate: bfloat16 [16, 1024, 7168], P('expert', 'section'), may hold values from -0.0625 to 0.0625
- w_up: bfloat16 [16, 1024, 7168], P('expert', 'section'), may hold values from -0.0625 to 0.0625
- w_down: bfloat16 [16, 1024, 7168], P('expert', 'section'), may hold values from -0.1875 to 0.1875
Outputs:
- mixed: bfloat16 [384, 7168], P('expert', 'section')
The draws below stay inside these ranges and needn't reach their ends.
Inputs may be any that keep to these rules, and one draw needn't show every extreme that they name: `expert_ids`: in each aligned block of 24 rows (the rows of one device), no expert is named by more than 16 of the block's pairs, a bound that some block reaches; a row names 8 different experts.
All inputs are finite; a program needn't handle non-finite values.
Results may differ from the reference program's by a relative error of at most 0.0057.
Values may be sent and summed in bfloat16 or wider, within the bound.
A program may use at most 128 MiB of HBM per device.

```python
import math
import jax
import jax.numpy as jnp
import numpy as np
from jax import lax

D = 7168
HID = 1024
TOP = 8
TOK_DEV = 24
EXPERTS = 16
TOKENS = 384
CAP = 16
N_SECTION = 2
N_EXPERT = 16


def shard_levels(rng, dims, pieces, smallest, largest):
    factor_of, own = 1.0, jax.random.fold_in(rng, 6)
    for position, parts in pieces:
        steps = jnp.exp(jax.random.uniform(jax.random.fold_in(own, position), (parts,), jnp.float32, smallest / len(pieces), largest / len(pieces)))
        factor_of = factor_of * jnp.repeat(steps, dims[position] // parts).reshape([-1 if axis == position else 1 for axis in range(len(dims))])
    return factor_of


def assign_block(stream_key, own, number, rows, number_of, top, most, skew):
    sequence = jax.random.permutation(stream_key, number_of)
    crowded, ordinary = portions_of(number_of, rows * top, most, skew, True), portions_of(number_of, rows * top, most, skew, False)
    places = jnp.arange(number_of)

    def named(sizes, rotation):
        used = int((sizes > 0).sum())
        fixed = max(1, used // 4)
        shifted = fixed + (places - fixed + rotation * (used - fixed)) % max(1, number_of - fixed)
        return jnp.zeros((number_of,), jnp.int32).at[sequence[jnp.where(places < fixed, places, shifted)]].set(jnp.asarray(sizes, jnp.int32))

    sizes = jnp.where(number % 4 == 0, named(crowded, number // 4), named(ordinary, number - number // 4 - 1))
    mixed = jax.random.permutation(jax.random.fold_in(own, 3), number_of)
    donor, sink = mixed[0:number_of // 2 * 2:2], mixed[1:number_of // 2 * 2:2]
    room = jnp.minimum(sizes[donor] - 1, most - sizes[sink]) // 2
    room = jnp.where((donor == sequence[0]) | (sink == sequence[0]) | (sizes[sink] == 0), 0, jnp.maximum(room, 0))
    shifted = jax.random.randint(jax.random.fold_in(own, 4), (number_of // 2,), 0, 1 << 20) % (room + 1)
    sizes = sizes.at[donor].add(-shifted).at[sink].add(shifted)
    members = jnp.searchsorted(jnp.cumsum(sizes), jnp.arange(rows * top), side="right").astype(jnp.int32)
    table = members.reshape(top, rows).T
    table = table[jax.random.permutation(jax.random.fold_in(own, 1), rows)]
    rotation = jax.random.randint(jax.random.fold_in(own, 2), (rows, 1), 0, top)
    return jnp.take_along_axis(table, (jnp.arange(top)[None, :] + rotation) % top, axis=1)


def portions_of(count, total, reach, skew, full):
    weights = [(1 << 20) // math.isqrt(rank ** skew) + 1 for rank in range(1, count + 1)]
    largest = reach if full else min(reach, max(-(-total // count), total * weights[0] // sum(weights)))
    least = 1 if total - largest >= count - 1 else 0
    counts, spare = [largest] + [least] * (count - 1), total - largest - least * (count - 1)
    while spare > 0:
        candidates = [i for i in range(1, count) if counts[i] < largest] or [i for i in range(1, count) if counts[i] < reach]
        mass, budget = sum([weights[i] for i in candidates]), spare
        for i in candidates:
            extra = min(reach - counts[i], max(1, budget * weights[i] // mass), spare)
            counts[i] = counts[i] + extra
            spare = spare - extra
    return np.array(counts)


def bell_draw(stream_key, dims, spread, bound, pieces=(), kind=jnp.bfloat16):
    result = spread * jax.random.normal(stream_key, dims, jnp.float32)
    if pieces:
        result = result * shard_levels(stream_key, dims, pieces, -0.22, 0.18)
    return jnp.clip(result, -bound, bound).astype(kind)


def setup_inputs(seed: int = 0) -> dict:
    splits = jax.random.split(jax.random.key(seed), 7)
    tokens = bell_draw(splits[0], (TOKENS, D), 1.0, 6.0, ((0, 16), (1, 2)))
    expert_ids_keys = jax.random.split(jax.random.fold_in(splits[1], 1), TOKENS // TOK_DEV)
    expert_ids_turns = jax.random.permutation(jax.random.fold_in(splits[1], 3), TOKENS // TOK_DEV)
    expert_ids = jax.vmap(lambda own, number: assign_block(jax.random.fold_in(splits[1], 2), own, number, TOK_DEV, EXPERTS, TOP, CAP, 2))(expert_ids_keys, expert_ids_turns).reshape((TOKENS, TOP))
    gate_weights = jnp.clip(0.099609375 + 0.49804688 * jax.random.uniform(splits[2], (TOKENS, TOP), jnp.float32) ** shard_levels(splits[2], (TOKENS, TOP), ((0, 16),), -0.2, 0.2), 0.099609375, 0.59765625).astype(jnp.bfloat16)
    w_gate = bell_draw(splits[3], (EXPERTS, HID, D), D ** -0.5, 0.0625, ((0, 16), (1, 2)))
    w_up = bell_draw(splits[4], (EXPERTS, HID, D), D ** -0.5, 0.0625, ((0, 16), (1, 2)))
    w_down = bell_draw(splits[5], (EXPERTS, HID, D), HID ** -0.5, 0.1875, ((0, 16), (1, 2)))
    return dict(tokens=tokens, expert_ids=expert_ids, gate_weights=gate_weights, w_gate=w_gate, w_up=w_up, w_down=w_down)


def expert_apply(args):
    inputs, gate_mat, up_mat, down_mat = args
    width = HID // N_SECTION
    total = jnp.zeros((inputs.shape[0], D), jnp.float32)
    for piece in range(N_SECTION):
        lower = piece * width
        gated = jnp.dot(inputs, gate_mat[lower:lower + width, :].T, preferred_element_type=jnp.float32)
        upward = jnp.dot(inputs, up_mat[lower:lower + width, :].T, preferred_element_type=jnp.float32)
        hidden = (jax.nn.silu(gated) * upward).astype(jnp.bfloat16)
        partial_value = jnp.dot(hidden, down_mat[lower:lower + width, :], preferred_element_type=jnp.float32).astype(jnp.bfloat16)
        total = total + partial_value.astype(jnp.float32)
    return total


def reference(tokens, expert_ids, gate_weights, w_gate, w_up, w_down):
    pairs = TOK_DEV * TOP
    chosen = expert_ids.reshape(N_EXPERT, pairs)
    onehot = (chosen[:, :, None] == jnp.arange(EXPERTS, dtype=jnp.int32)[None, None, :]).astype(jnp.int32)
    order_rank = jnp.cumsum(onehot, axis=1) - 1
    slot_index = jnp.sum(order_rank * onehot, axis=2).astype(jnp.int32)
    source = jnp.broadcast_to(jnp.arange(N_EXPERT, dtype=jnp.int32)[:, None], (N_EXPERT, pairs))
    token_row = jnp.broadcast_to((jnp.arange(pairs, dtype=jnp.int32) // TOP)[None, :], (N_EXPERT, pairs))
    table = jnp.full((EXPERTS, N_EXPERT, CAP), TOK_DEV, jnp.int32)
    table = table.at[chosen, source, slot_index].set(token_row)
    blocks = tokens.reshape(N_EXPERT, TOK_DEV, D)
    padded = jnp.concatenate([blocks, jnp.zeros((N_EXPERT, 1, D), blocks.dtype)], axis=1)
    buffer = padded[jnp.arange(N_EXPERT, dtype=jnp.int32)[None, :, None], table]
    flat = buffer.reshape(EXPERTS, N_EXPERT * CAP, D)
    results = lax.map(expert_apply, (flat, w_gate, w_up, w_down))
    results = results.reshape(EXPERTS, N_EXPERT, CAP, D)
    picked = results[chosen, source, slot_index]
    scales = gate_weights.reshape(N_EXPERT, pairs).astype(jnp.float32)
    weighted = picked * scales[:, :, None]
    summed = jnp.sum(weighted.reshape(N_EXPERT, TOK_DEV, TOP, D), axis=2)
    return summed.reshape(TOKENS, D).astype(jnp.bfloat16)
```

```python
import jax
import jax.numpy as jnp
from jax import lax
from jax.sharding import PartitionSpec as P


def on_device(tokens, expert_ids, gate_weights, w_gate, w_up, w_down):
    me = lax.axis_index("expert")
    contract_last = (((1,), (1,)), ((), ()))
    rows = lax.all_gather(tokens, "section", axis=1, tiled=True)
    inputs = lax.all_gather(rows, "expert", axis=0, tiled=True)
    ids = lax.all_gather(expert_ids, "expert", axis=0, tiled=True)
    weights = lax.all_gather(gate_weights, "expert", axis=0, tiled=True)
    scale = jnp.sum(
        jnp.where(ids == me, weights.astype(jnp.float32), 0.0), axis=1, keepdims=True
    )
    gated = lax.dot_general(inputs, w_gate[0], contract_last, preferred_element_type=jnp.float32)
    upward = lax.dot_general(inputs, w_up[0], contract_last, preferred_element_type=jnp.float32)
    hidden = (jax.nn.silu(gated) * upward).astype(jnp.bfloat16)
    partial_value = jnp.dot(hidden, w_down[0], preferred_element_type=jnp.float32)
    weighted = (partial_value * scale).astype(jnp.bfloat16)
    across = lax.psum_scatter(weighted, "section", scatter_dimension=1, tiled=True)
    return lax.psum_scatter(across, "expert", scatter_dimension=0, tiled=True)


def solution(mesh):
    placed = (
        P("expert", "section"),
        P("expert", None),
        P("expert", None),
        P("expert", "section", None),
        P("expert", "section", None),
        P("expert", "section", None),
    )
    return jax.shard_map(
        on_device, mesh=mesh, in_specs=placed, out_specs=P("expert", "section"), check_vma=False
    )
```

```python
import functools
import jax
import jax.numpy as jnp
from jax import lax
from jax.experimental import pallas as pl
from jax.experimental.pallas import tpu as pltpu
from jax.sharding import PartitionSpec as P

MESH = pl.DeviceIdType.MESH
F32 = jnp.float32
BF16 = jnp.bfloat16
NZ = 4
N_PAIR = 2 * NZ
N_DEV = 2 * N_PAIR


def moe_kernel(
    tok_ref, ids_ref, gw_ref, wg_hbm, wu_hbm, wd_hbm, out_ref,
    wg, wu, wd, rows_x, tok_sib, table, gated, upward, hidden, scale,
    part, core_out, core_in, first_out, first_in, second_out, second_in,
    total, line_out, line_in, fin_out, fin_in,
    sem_w, sem_tok, sem_tab_s, sem_tab_r,
    sem_line_s, sem_line_r, sem_d1_s, sem_d1_r, sem_d2_s, sem_d2_r, sem_core_s, sem_core_r,
    sem_cx_s, sem_cx_r, sem_f_s, sem_f_r, sem_s_s, sem_s_r, sem_l_s, sem_l_r, sem_fin,
):
    count, _ = tok_ref.shape
    block = 2 * count
    chunk = rows_x.shape[2]
    me = lax.axis_index("expert")
    x = lax.axis_index("section")
    z, y, c = me // 4, (me // 2) % 2, me % 2

    def dev(x_, z_, y_, c_):
        return {"section": x_, "expert": z_ * 4 + y_ * 2 + c_}

    sibling = dev(x, z, y, 1 - c)
    x_peer = dev(1 - x, z, y, c)
    y_peer = dev(x, z, 1 - y, c)

    def remote(src, dst, s, r, to):
        return pltpu.make_async_remote_copy(
            src_ref=src, dst_ref=dst, send_sem=s, recv_sem=r, device_id=to, device_id_type=MESH
        )

    weight_copies = [
        pltpu.make_async_copy(wg_hbm.at[0], wg, sem_w.at[0]),
        pltpu.make_async_copy(wu_hbm.at[0], wu, sem_w.at[1]),
        pltpu.make_async_copy(wd_hbm.at[0], wd, sem_w.at[2]),
    ]
    for copy in weight_copies:
        copy.start()

    barrier = pltpu.get_barrier_semaphore()
    for step in range(1, N_DEV):
        pl.semaphore_signal(
            barrier, inc=1, device_id={"section": x, "expert": (me + step) % N_DEV},
            device_id_type=MESH,
        )
    pl.semaphore_signal(barrier, inc=1, device_id=x_peer, device_id_type=MESH)
    pl.semaphore_wait(barrier, N_DEV)

    tok_copy = remote(tok_ref, tok_sib, sem_tok.at[0], sem_tok.at[1], sibling)
    tok_copy.start()

    lane = lax.broadcasted_iota(jnp.int32, (count, 128), 1)
    weights = jnp.zeros((count, 128), F32)
    for k in range(ids_ref.shape[1]):
        weights = weights + jnp.where(lane == ids_ref[:, k:k + 1], gw_ref[:, k:k + 1].astype(F32), 0.0)
    table[me] = weights

    tok_copy.wait()
    for j in range(4):
        cols = slice(j * chunk, (j + 1) * chunk)
        mine, other = tok_ref[:, cols], tok_sib[:, cols]
        lower = jnp.where(c == 0, mine.astype(F32), other.astype(F32)).astype(BF16)
        upper = jnp.where(c == 0, other.astype(F32), mine.astype(F32)).astype(BF16)
        rows_x[x * 4 + j, pl.ds(pl.multiple_of((z * 2 + y) * block, block), block), :] = (
            jnp.concatenate([lower, upper], axis=0)
        )

    def spot(h, x_, z_, y_):
        return rows_x.at[
            x_ * 4 + c * 2 + h, pl.ds(pl.multiple_of((z_ * 2 + y_) * block, block), block), :
        ]

    def label(h, x_, z_, y_):
        return h * 4 * NZ + x_ * N_PAIR + z_ * 2 + y_

    def along_line(h, z_, up):
        place = spot(h, x, z_, y)
        to = dev(x, z + 1 if up else z - 1, y, c)
        return remote(
            place, place, sem_line_s.at[h * 2 * NZ + (0 if up else NZ) + z_],
            sem_line_r.at[h * NZ + z_], to,
        )

    def first_hop(h, z_):
        place = spot(h, x, z_, y)
        return remote(
            place, place, sem_d1_s.at[h * NZ + z_], sem_d1_r.at[h * NZ + z_],
            y_peer if h == 0 else x_peer,
        )

    def first_arrived(h, z_):
        return (h, x, z_, 1 - y) if h == 0 else (h, 1 - x, z_, y)

    def first_wait(h, z_):
        place = spot(*first_arrived(h, z_))
        remote(place, place, sem_d1_s.at[h * NZ + z_], sem_d1_r.at[h * NZ + z_], sibling).wait_recv()

    def second_hop(h, z_, own):
        place = spot(h, x, z_, y) if own else spot(*first_arrived(h, z_))
        i = h * 2 * NZ + (0 if own else NZ) + z_
        return remote(
            place, place, sem_d2_s.at[i], sem_d2_r.at[i], x_peer if h == 0 else y_peer
        )

    def second_arrived(h, z_, own):
        if h == 0:
            return (h, 1 - x, z_, y if own else 1 - y)
        return (h, x if own else 1 - x, z_, 1 - y)

    def second_wait(h, z_, own):
        place = spot(*second_arrived(h, z_, own))
        i = h * 2 * NZ + (0 if own else NZ) + z_
        remote(place, place, sem_d2_s.at[i], sem_d2_r.at[i], sibling).wait_recv()

    def to_sibling(h, x_, z_, y_):
        place = spot(h, x_, z_, y_)
        i = label(h, x_, z_, y_)
        return remote(place, place, sem_core_s.at[i], sem_core_r.at[i], sibling)

    def from_sibling(h, x_, z_, y_):
        place = rows_x.at[
            x_ * 4 + (1 - c) * 2 + h, pl.ds(pl.multiple_of((z_ * 2 + y_) * block, block), block), :
        ]
        i = label(h, x_, z_, y_)
        return remote(place, place, sem_core_s.at[i], sem_core_r.at[i], sibling)

    def level(k, fn):
        if k == 0:
            fn(z, None)
            return

        @pl.when(z - k >= 0)
        def _():
            fn(z - k, True)

        @pl.when(z + k < NZ)
        def _():
            fn(z + k, False)

    for h in range(2):
        @pl.when(z < NZ - 1)
        def _():
            along_line(h, z, True).start()

        @pl.when(z > 0)
        def _():
            along_line(h, z, False).start()

        first_hop(h, z).start()
        second_hop(h, z, True).start()

    for step in range(1, N_DEV):
        peer = (me + step) % N_DEV
        remote(
            table.at[me], table.at[me], sem_tab_s.at[step], sem_tab_r.at[me],
            {"section": x, "expert": peer},
        ).start()

    for k in range(1, NZ + 1):
        for h in range(2):
            if k < NZ:
                def arrived(z_, up):
                    place = spot(h, x, z_, y)
                    remote(
                        place, place, sem_line_s.at[h * 2 * NZ + z_], sem_line_r.at[h * NZ + z_],
                        sibling,
                    ).wait_recv()
                    if up:
                        @pl.when(z < NZ - 1)
                        def _():
                            along_line(h, z_, True).start()
                    else:
                        @pl.when(z > 0)
                        def _():
                            along_line(h, z_, False).start()
                    first_hop(h, z_).start()
                    second_hop(h, z_, True).start()
                    to_sibling(h, x, z_, y).start()

                level(k, arrived)
        for h in range(2):
            def arrived_first(z_, up):
                first_wait(h, z_)
                second_hop(h, z_, False).start()
                to_sibling(*first_arrived(h, z_)).start()

            level(k - 1, arrived_first)

    for own, k in ((True, 0), (True, 1), (False, 0), (True, 2), (False, 1), (True, 3), (False, 2), (False, 3)):
        for h in range(2):
            def arrived_second(z_, up):
                second_wait(h, z_, own)
                to_sibling(*second_arrived(h, z_, own)).start()

            level(k, arrived_second)

    for h in range(2):
        for x_ in range(2):
            for z_ in range(NZ):
                for y_ in range(2):
                    @pl.when(jnp.logical_or(x_ != x, jnp.logical_or(z_ != z, y_ != y)))
                    def _():
                        from_sibling(h, x_, z_, y_).wait_recv()

    weight_copies[0].wait()
    weight_copies[1].wait()
    contract_last = (((1,), (1,)), ((), ()))
    gated[...] = jnp.zeros_like(gated)
    upward[...] = jnp.zeros_like(upward)

    def up_step(q, carry):
        cols = pl.ds(pl.multiple_of(q * chunk, 128), chunk)
        inputs = rows_x[q]
        gated[...] += lax.dot_general(inputs, wg[:, cols], contract_last, preferred_element_type=F32)
        upward[...] += lax.dot_general(inputs, wu[:, cols], contract_last, preferred_element_type=F32)
        return carry

    lax.fori_loop(0, 8, up_step, 0)
    value = gated[...]
    hidden[...] = (value / (1.0 + jnp.exp(-value)) * upward[...]).astype(BF16)

    for step in range(1, N_DEV):
        peer = (me + N_DEV - step) % N_DEV
        remote(
            table.at[peer], table.at[peer], sem_tab_s.at[step], sem_tab_r.at[peer], sibling
        ).wait_recv()
    lane = lax.broadcasted_iota(jnp.int32, (N_DEV * count, 128), 1)
    every = jnp.concatenate([table[i] for i in range(N_DEV)], axis=0)
    scale[...] = jnp.broadcast_to(
        jnp.sum(jnp.where(lane == me, every, 0.0), axis=1, keepdims=True), scale.shape
    )

    weight_copies[2].wait()
    n_rows = N_PAIR * block

    def down(x_, c_, h):
        q = x_ * 4 + c_ * 2 + h
        cols = pl.ds(pl.multiple_of(q * chunk, 128), chunk)
        return jnp.dot(hidden[...], wd[:, cols], preferred_element_type=F32) * scale[:, 0:1]

    def core_copy(x_, h):
        i = x_ * 2 + h
        return remote(core_out.at[i], core_in.at[i], sem_cx_s.at[i], sem_cx_r.at[i], sibling)

    order = ((1 - x, 0), (1 - x, 1), (x, 1), (x, 0))

    def order_step(i):
        return jnp.where(i < 2, 1 - x, x), jnp.where(jnp.logical_or(i == 1, i == 2), 1, 0)

    def send_step(i, carry):
        x_, h = order_step(i)
        core_out[x_ * 2 + h] = down(x_, 1 - c, h).astype(BF16)
        core_copy(x_, h).start()
        return carry

    lax.fori_loop(0, 4, send_step, 0)

    def keep_step(i, carry):
        x_, h = order_step(i)
        part[x_ * 2 + h] = down(x_, c, h)
        return carry

    lax.fori_loop(0, 4, keep_step, 0)

    def span(z_, y_):
        return pl.ds(pl.multiple_of((z_ * 2 + y_) * block, block), block)

    def chip_sum(h, x_, z_, y_):
        i = x_ * 2 + h
        return part[i, span(z_, y_), :] + core_in[i, span(z_, y_), :].astype(F32)

    def first_slot(h, other, z_):
        return h * 2 * NZ + (NZ if other else 0) + z_

    def first_copy(h, other, z_):
        i = first_slot(h, other, z_)
        return remote(
            first_out.at[i], first_in.at[i], sem_f_s.at[i], sem_f_r.at[i],
            x_peer if h == 0 else y_peer,
        )

    def second_copy(h, z_):
        i = h * NZ + z_
        return remote(
            second_out.at[i], second_in.at[i], sem_s_s.at[i], sem_s_r.at[i],
            y_peer if h == 0 else x_peer,
        )

    zs = range(NZ)
    for g, (x_, h) in enumerate(order):
        core_copy(x_, h).wait_recv()
        if g == 0:
            for other in (True, False):
                for z_ in zs:
                    first_out[first_slot(0, other, z_)] = chip_sum(
                        0, 1 - x, z_, 1 - y if other else y
                    ).astype(BF16)
                    first_copy(0, other, z_).start()
        elif g in (1, 2):
            other = g == 1
            for z_ in zs:
                first_out[first_slot(1, other, z_)] = chip_sum(
                    1, 1 - x if other else x, z_, 1 - y
                ).astype(BF16)
                first_copy(1, other, z_).start()

    for z_ in zs:
        for h in range(2):
            first_copy(h, True, z_).wait_recv()
            mine = chip_sum(0, x, z_, 1 - y) if h == 0 else chip_sum(1, 1 - x, z_, y)
            second_out[h * NZ + z_] = (mine + first_in[first_slot(h, True, z_)].astype(F32)).astype(BF16)
            second_copy(h, z_).start()
    for z_ in zs:
        for h in range(2):
            first_copy(h, False, z_).wait_recv()
            second_copy(h, z_).wait_recv()
            total[h * NZ + z_] = (
                chip_sum(h, x, z_, y)
                + first_in[first_slot(h, False, z_)].astype(F32)
                + second_in[h * NZ + z_].astype(F32)
            )

    near_up = z < NZ // 2

    def line_copy(h, up, dest):
        i = h * 2 * NZ + up * NZ + dest
        return remote(
            line_out.at[i], line_in.at[i], sem_l_s.at[i], sem_l_r.at[i],
            dev(x, jnp.where(up == 1, z + 1, z - 1), y, c),
        )

    def line_state(k, turn):
        up = jnp.where(near_up, 1 - turn, turn)
        dest = jnp.where(up == 1, NZ - 1 - k, k)
        active = jnp.where(up == 1, dest - z, z - dest) > 0
        feeds = jnp.where(up == 1, z, NZ - 1 - z) > 0
        return up, dest, active, feeds

    for k in range(NZ - 1):
        for turn in range(2):
            up, dest, active, feeds = line_state(k, turn)

            @pl.when(jnp.logical_and(active, feeds))
            def _():
                for h in range(2):
                    i = h * 2 * NZ + up * NZ + dest
                    line_copy(h, up, dest).wait_recv()
                    line_out[i] = (total[h * NZ + dest] + line_in[i].astype(F32)).astype(BF16)
                    line_copy(h, up, dest).start()

            @pl.when(jnp.logical_and(active, jnp.logical_not(feeds)))
            def _():
                for h in range(2):
                    i = h * 2 * NZ + up * NZ + dest
                    line_out[i] = total[h * NZ + dest].astype(BF16)
                    line_copy(h, up, dest).start()

    for h in range(2):
        for up in range(2):
            @pl.when((z > 0) if up == 1 else (z < NZ - 1))
            def _():
                line_copy(h, up, z).wait_recv()
                total[h * NZ + z] += line_in[h * 2 * NZ + up * NZ + z].astype(F32)

    fin_copy = remote(fin_out, fin_in, sem_fin.at[0], sem_fin.at[1], sibling)
    halves = []
    for h in range(2):
        whole = total[h * NZ + z]
        lower, upper = whole[:count], whole[count:]
        fin_out[h] = jnp.where(c == 0, upper, lower).astype(BF16)
        halves.append(jnp.where(c == 0, lower, upper).astype(BF16))
    fin_copy.start()
    fin_copy.wait()
    for h in range(2):
        theirs = fin_in[h].astype(F32)
        mine = halves[h].astype(F32)
        out_ref[:, h * chunk:(h + 1) * chunk] = jnp.where(c == 0, mine, theirs).astype(BF16)
        out_ref[:, (2 + h) * chunk:(3 + h) * chunk] = jnp.where(c == 0, theirs, mine).astype(BF16)

    for step in range(1, N_DEV):
        remote(
            table.at[me], table.at[me], sem_tab_s.at[step], sem_tab_r.at[me], sibling
        ).wait_send()
    for h in range(2):
        for k in range(NZ):
            def sent(z_, up):
                if up is None or up:
                    @pl.when(z < NZ - 1)
                    def _():
                        along_line(h, z_, True).wait_send()
                if not up:
                    @pl.when(z > 0)
                    def _():
                        along_line(h, z_, False).wait_send()

            level(k, sent)
        for z_ in zs:
            first_hop(h, z_).wait_send()
            second_hop(h, z_, True).wait_send()
            second_hop(h, z_, False).wait_send()
            for x_ in range(2):
                for y_ in range(2):
                    @pl.when(jnp.logical_or(x_ != x, jnp.logical_or(z_ != z, y_ != y)))
                    def _():
                        to_sibling(h, x_, z_, y_).wait_send()
            first_copy(h, True, z_).wait_send()
            first_copy(h, False, z_).wait_send()
            second_copy(h, z_).wait_send()
        for x_ in range(2):
            core_copy(x_, h).wait_send()
    for k in range(NZ - 1):
        for turn in range(2):
            up, dest, active, feeds = line_state(k, turn)

            @pl.when(active)
            def _():
                for h in range(2):
                    line_copy(h, up, dest).wait_send()


def fused(tokens, expert_ids, gate_weights, w_gate, w_up, w_down):
    count, share = tokens.shape
    hid, width = w_gate.shape[1:]
    chunk = share // 4
    block = 2 * count
    n_rows = N_PAIR * block
    dma = pltpu.SemaphoreType.DMA
    vmem = lambda shape, dtype: pltpu.VMEM(shape, dtype)
    blocks = lambda n: pltpu.VMEM((n, block, chunk), BF16)
    return pl.pallas_call(
        moe_kernel,
        out_shape=jax.ShapeDtypeStruct((count, share), BF16),
        in_specs=[pl.BlockSpec(memory_space=pltpu.VMEM)] * 3 + [pl.BlockSpec(memory_space=pl.ANY)] * 3,
        out_specs=pl.BlockSpec(memory_space=pltpu.VMEM),
        scratch_shapes=[
            vmem((hid, width), BF16), vmem((hid, width), BF16), vmem((hid, width), BF16),
            vmem((8, n_rows, chunk), BF16), vmem((count, share), BF16),
            vmem((N_DEV, count, 128), F32),
            vmem((n_rows, hid), F32), vmem((n_rows, hid), F32), vmem((n_rows, hid), BF16),
            vmem((n_rows, 128), F32),
            vmem((4, n_rows, chunk), F32), vmem((4, n_rows, chunk), BF16), vmem((4, n_rows, chunk), BF16),
            blocks(4 * NZ), blocks(4 * NZ), blocks(2 * NZ), blocks(2 * NZ),
            vmem((2 * NZ, block, chunk), F32), blocks(4 * NZ), blocks(4 * NZ),
            vmem((2, count, chunk), BF16), vmem((2, count, chunk), BF16),
            dma((3,)), dma((2,)), dma((N_DEV,)), dma((N_DEV,)),
            dma((4 * NZ,)), dma((2 * NZ,)), dma((2 * NZ,)), dma((2 * NZ,)),
            dma((4 * NZ,)), dma((4 * NZ,)), dma((8 * NZ,)), dma((8 * NZ,)),
            dma((4,)), dma((4,)), dma((4 * NZ,)), dma((4 * NZ,)), dma((2 * NZ,)), dma((2 * NZ,)),
            dma((4 * NZ,)), dma((4 * NZ,)), dma((2,)),
        ],
        compiler_params=pltpu.CompilerParams(
            collective_id=0, has_side_effects=True, vmem_limit_bytes=60 * 1024 * 1024
        ),
        cost_estimate=pl.CostEstimate(
            flops=6 * n_rows * hid * width, bytes_accessed=6 * hid * width,
            transcendentals=n_rows * hid,
        ),
    )(tokens, expert_ids, gate_weights, w_gate, w_up, w_down)


def on_device(tokens, expert_ids, gate_weights, w_gate, w_up, w_down):
    n_dest = lax.axis_size("expert")
    token_count = tokens.shape[0]
    chosen = expert_ids.shape[1]
    width = w_gate.shape[2]
    capacity = min(token_count, token_count * chosen * 4 // (3 * n_dest))
    flat_ids = expert_ids.reshape(-1)
    onehot = (flat_ids[:, None] == jnp.arange(n_dest, dtype=jnp.int32)[None, :]).astype(jnp.int32)
    order_rank = jnp.cumsum(onehot, axis=0) - 1
    slot_index = jnp.sum(order_rank * onehot, axis=1)
    target = flat_ids * capacity + slot_index
    token_of = jnp.arange(token_count * chosen, dtype=jnp.int32) // chosen
    matches = (jnp.arange(n_dest * capacity, dtype=jnp.int32)[:, None] == target[None, :]).astype(
        jnp.bfloat16
    )
    token_map = (token_of[:, None] == jnp.arange(token_count, dtype=jnp.int32)[None, :]).astype(
        jnp.bfloat16
    )
    dispatch_matrix = jnp.dot(matches, token_map, preferred_element_type=jnp.float32).astype(
        jnp.bfloat16
    )
    scaled_map = token_map * gate_weights.reshape(-1)[:, None]
    combine_matrix = jnp.dot(scaled_map.T, matches.T, preferred_element_type=jnp.float32).astype(
        jnp.bfloat16
    )
    contract_last = (((1,), (1,)), ((), ()))
    features = lax.all_gather(tokens, "section", axis=1, tiled=True)
    send_rows = jnp.dot(dispatch_matrix, features, preferred_element_type=jnp.float32).astype(
        jnp.bfloat16
    )
    send_rows = send_rows.reshape(n_dest, capacity, width)
    received = lax.all_to_all(send_rows, "expert", split_axis=0, concat_axis=0, tiled=True)
    inputs = received.reshape(-1, width)
    gated = lax.dot_general(inputs, w_gate[0], contract_last, preferred_element_type=jnp.float32)
    upward = lax.dot_general(inputs, w_up[0], contract_last, preferred_element_type=jnp.float32)
    hidden = (jax.nn.silu(gated) * upward).astype(jnp.bfloat16)
    partial_value = jnp.dot(hidden, w_down[0], preferred_element_type=jnp.float32).astype(
        jnp.bfloat16
    )
    partial_value = partial_value.reshape((received.shape[0], received.shape[1], width))
    returned = lax.all_to_all(partial_value, "expert", split_axis=0, concat_axis=0, tiled=True)
    weighted = jnp.dot(
        combine_matrix, returned.reshape(-1, width), preferred_element_type=jnp.float32
    )
    return lax.psum_scatter(weighted, "section", scatter_dimension=1, tiled=True).astype(
        jnp.bfloat16
    )


def solution(mesh):
    placed = (
        P("expert", "section"),
        P("expert", None),
        P("expert", None),
        P("expert", "section", None),
        P("expert", "section", None),
        P("expert", "section", None),
    )
    whole_kernel = mesh.shape["section"] == 2 and mesh.shape["expert"] == N_DEV
    return jax.shard_map(
        fused if whole_kernel else on_device, mesh=mesh, in_specs=placed, out_specs=P("expert", "section"), check_vma=False
    )
```

```python
import functools
import jax
import jax.numpy as jnp
from jax import lax
from jax.experimental import pallas as pl
from jax.experimental.pallas import tpu as pltpu
from jax.sharding import PartitionSpec as P

MESH = pl.DeviceIdType.MESH
F32 = jnp.float32
BF16 = jnp.bfloat16
NZ = 4
N_PAIR = 2 * NZ
N_DEV = 2 * N_PAIR


def moe_kernel(
    tok_ref, ids_ref, gw_ref, wg_hbm, wu_hbm, wd_hbm, out_ref,
    wg, wu, wd, rows_x, tok_sib, table, gated, upward, hidden, scale,
    part, core_out, core_in, first_out, first_in, second_out, second_in,
    total, line_out, line_in, fin_out, fin_in,
    sem_w, sem_tok, sem_tab_s, sem_tab_r,
    sem_line_s, sem_line_r, sem_d1_s, sem_d1_r, sem_d2_s, sem_d2_r, sem_core_s, sem_core_r,
    sem_cx_s, sem_cx_r, sem_f_s, sem_f_r, sem_s_s, sem_s_r, sem_l_s, sem_l_r, sem_fin,
):
    count, _ = tok_ref.shape
    block = 2 * count
    chunk = rows_x.shape[2]
    me = lax.axis_index("expert")
    x = lax.axis_index("section")
    z, y, c = me // 4, (me // 2) % 2, me % 2

    def dev(x_, z_, y_, c_):
        return {"section": x_, "expert": z_ * 4 + y_ * 2 + c_}

    sibling = dev(x, z, y, 1 - c)
    x_peer = dev(1 - x, z, y, c)
    y_peer = dev(x, z, 1 - y, c)

    def remote(src, dst, s, r, to):
        return pltpu.make_async_remote_copy(
            src_ref=src, dst_ref=dst, send_sem=s, recv_sem=r, device_id=to, device_id_type=MESH
        )

    def row_at(z_, y_):
        return pl.ds(pl.multiple_of((y_ * NZ + z_) * block, block), block)

    weight_copies = [
        pltpu.make_async_copy(wg_hbm.at[0], wg, sem_w.at[0]),
        pltpu.make_async_copy(wu_hbm.at[0], wu, sem_w.at[1]),
        pltpu.make_async_copy(wd_hbm.at[0], wd, sem_w.at[2]),
    ]
    for copy in weight_copies:
        copy.start()

    barrier = pltpu.get_barrier_semaphore()
    for step in range(1, N_DEV):
        pl.semaphore_signal(
            barrier, inc=1, device_id={"section": x, "expert": (me + step) % N_DEV},
            device_id_type=MESH,
        )
    pl.semaphore_signal(barrier, inc=1, device_id=x_peer, device_id_type=MESH)
    pl.semaphore_wait(barrier, N_DEV)

    tok_copy = remote(tok_ref, tok_sib, sem_tok.at[0], sem_tok.at[1], sibling)
    tok_copy.start()

    lane = lax.broadcasted_iota(jnp.int32, (count, 128), 1)
    weights = jnp.zeros((count, 128), F32)
    for k in range(ids_ref.shape[1]):
        weights = weights + jnp.where(lane == ids_ref[:, k:k + 1], gw_ref[:, k:k + 1].astype(F32), 0.0)
    table[me] = weights

    tok_copy.wait()
    for j in range(4):
        cols = slice(j * chunk, (j + 1) * chunk)
        mine, other = tok_ref[:, cols], tok_sib[:, cols]
        lower = jnp.where(c == 0, mine.astype(F32), other.astype(F32)).astype(BF16)
        upper = jnp.where(c == 0, other.astype(F32), mine.astype(F32)).astype(BF16)
        rows_x[x * 4 + j, row_at(z, y), :] = (
            jnp.concatenate([lower, upper], axis=0)
        )

    def spot(h, x_, z_, y_):
        return rows_x.at[
            x_ * 4 + c * 2 + h, row_at(z_, y_), :
        ]

    def label(h, x_, z_, y_):
        return h * 4 * NZ + x_ * N_PAIR + z_ * 2 + y_

    def along_line(h, z_, up):
        place = spot(h, x, z_, y)
        to = dev(x, z + 1 if up else z - 1, y, c)
        return remote(
            place, place, sem_line_s.at[h * 2 * NZ + (0 if up else NZ) + z_],
            sem_line_r.at[h * NZ + z_], to,
        )

    def first_hop(h, z_):
        place = spot(h, x, z_, y)
        return remote(
            place, place, sem_d1_s.at[h * NZ + z_], sem_d1_r.at[h * NZ + z_],
            y_peer if h == 0 else x_peer,
        )

    def first_arrived(h, z_):
        return (h, x, z_, 1 - y) if h == 0 else (h, 1 - x, z_, y)

    def first_wait(h, z_):
        place = spot(*first_arrived(h, z_))
        remote(place, place, sem_d1_s.at[h * NZ + z_], sem_d1_r.at[h * NZ + z_], sibling).wait_recv()

    def second_hop(h, z_, own):
        place = spot(h, x, z_, y) if own else spot(*first_arrived(h, z_))
        i = h * 2 * NZ + (0 if own else NZ) + z_
        return remote(
            place, place, sem_d2_s.at[i], sem_d2_r.at[i], x_peer if h == 0 else y_peer
        )

    def second_arrived(h, z_, own):
        if h == 0:
            return (h, 1 - x, z_, y if own else 1 - y)
        return (h, x if own else 1 - x, z_, 1 - y)

    def second_wait(h, z_, own):
        place = spot(*second_arrived(h, z_, own))
        i = h * 2 * NZ + (0 if own else NZ) + z_
        remote(place, place, sem_d2_s.at[i], sem_d2_r.at[i], sibling).wait_recv()

    def to_sibling(h, x_, z_, y_):
        place = spot(h, x_, z_, y_)
        i = label(h, x_, z_, y_)
        return remote(place, place, sem_core_s.at[i], sem_core_r.at[i], sibling)

    def from_sibling(h, x_, z_, y_):
        place = rows_x.at[
            x_ * 4 + (1 - c) * 2 + h, row_at(z_, y_), :
        ]
        i = label(h, x_, z_, y_)
        return remote(place, place, sem_core_s.at[i], sem_core_r.at[i], sibling)

    def level(k, fn):
        if k == 0:
            fn(z, None)
            return

        @pl.when(z - k >= 0)
        def _():
            fn(z - k, True)

        @pl.when(z + k < NZ)
        def _():
            fn(z + k, False)

    for h in range(2):
        @pl.when(z < NZ - 1)
        def _():
            along_line(h, z, True).start()

        @pl.when(z > 0)
        def _():
            along_line(h, z, False).start()

        first_hop(h, z).start()
        second_hop(h, z, True).start()

    for step in range(1, N_DEV):
        peer = (me + step) % N_DEV
        remote(
            table.at[me], table.at[me], sem_tab_s.at[step], sem_tab_r.at[me],
            {"section": x, "expert": peer},
        ).start()

    for k in range(1, NZ + 1):
        for h in range(2):
            if k < NZ:
                def arrived(z_, up):
                    place = spot(h, x, z_, y)
                    remote(
                        place, place, sem_line_s.at[h * 2 * NZ + z_], sem_line_r.at[h * NZ + z_],
                        sibling,
                    ).wait_recv()
                    if up:
                        @pl.when(z < NZ - 1)
                        def _():
                            along_line(h, z_, True).start()
                    else:
                        @pl.when(z > 0)
                        def _():
                            along_line(h, z_, False).start()
                    first_hop(h, z_).start()
                    second_hop(h, z_, True).start()
                    to_sibling(h, x, z_, y).start()

                level(k, arrived)
        for h in range(2):
            def arrived_first(z_, up):
                first_wait(h, z_)
                second_hop(h, z_, False).start()
                to_sibling(*first_arrived(h, z_)).start()

            level(k - 1, arrived_first)

    contract_last = (((1,), (1,)), ((), ()))
    gated[...] = jnp.zeros_like(gated)
    upward[...] = jnp.zeros_like(upward)
    weight_copies[0].wait()
    weight_copies[1].wait()
    half_rows = NZ * block

    def up_add(q, where):
        cols = pl.ds(pl.multiple_of(q * chunk, 128), chunk)
        inputs = rows_x[q, where, :]
        gated[where, :] += lax.dot_general(inputs, wg[:, cols], contract_last, preferred_element_type=F32)
        upward[where, :] += lax.dot_general(inputs, wu[:, cols], contract_last, preferred_element_type=F32)

    def up_all_rows(x_):
        def body(i, carry):
            up_add(x_ * 4 + i * 2, pl.ds(0, 2 * half_rows))
            return carry

        lax.fori_loop(0, 2, body, 0)

    def up_half_rows(y_):
        def body(i, carry):
            up_add(i * 2 + 1, pl.ds(pl.multiple_of(y_ * half_rows, half_rows), half_rows))
            return carry

        lax.fori_loop(0, 4, body, 0)

    def wait_sibling(h, x_, y_):
        for z_ in range(NZ):
            @pl.when(jnp.logical_or(x_ != x, jnp.logical_or(z_ != z, y_ != y)))
            def _():
                from_sibling(h, x_, z_, y_).wait_recv()

    def drain(items):
        for own, k in items:
            for h in range(2):
                def arrived_second(z_, up):
                    second_wait(h, z_, own)
                    to_sibling(*second_arrived(h, z_, own)).start()

                level(k, arrived_second)

    for y_ in (y, 1 - y):
        wait_sibling(0, x, y_)
    up_all_rows(x)
    drain(((True, 0), (True, 1), (False, 0), (True, 2)))
    for x_ in (x, 1 - x):
        wait_sibling(1, x_, y)
    up_half_rows(y)
    drain(((False, 1), (True, 3), (False, 2), (False, 3)))
    for y_ in (y, 1 - y):
        wait_sibling(0, 1 - x, y_)
    up_all_rows(1 - x)
    for x_ in (x, 1 - x):
        wait_sibling(1, x_, 1 - y)
    up_half_rows(1 - y)
    value = gated[...]
    hidden[...] = (value / (1.0 + jnp.exp(-value)) * upward[...]).astype(BF16)

    for step in range(1, N_DEV):
        peer = (me + N_DEV - step) % N_DEV
        remote(
            table.at[peer], table.at[peer], sem_tab_s.at[step], sem_tab_r.at[peer], sibling
        ).wait_recv()
    lane = lax.broadcasted_iota(jnp.int32, (N_DEV * count, 128), 1)
    every = jnp.concatenate([table[z_ * 4 + y_ * 2 + c_] for y_ in range(2) for z_ in range(NZ) for c_ in range(2)], axis=0)
    scale[...] = jnp.broadcast_to(
        jnp.sum(jnp.where(lane == me, every, 0.0), axis=1, keepdims=True), scale.shape
    )

    weight_copies[2].wait()
    n_rows = N_PAIR * block

    def down(x_, c_, h):
        q = x_ * 4 + c_ * 2 + h
        cols = pl.ds(pl.multiple_of(q * chunk, 128), chunk)
        return jnp.dot(hidden[...], wd[:, cols], preferred_element_type=F32) * scale[:, 0:1]

    def dest_at(j):
        a, b, d, e = ((3, 3, 0, 0), (2, 0, 3, 1), (1, 2, 1, 2), (0, 1, 2, 3))[j]
        return jnp.where(z == 0, a, jnp.where(z == 1, b, jnp.where(z == 2, d, e)))

    def core_copy(x_, h, z_, y_):
        i = x_ * 2 + h
        n = i * N_PAIR + z_ * 2 + y_
        return remote(
            core_out.at[i, row_at(z_, y_), :], core_in.at[i, row_at(z_, y_), :],
            sem_cx_s.at[n], sem_cx_r.at[n], sibling,
        )

    def order_step(i):
        return jnp.where(i < 2, 1 - x, x), jnp.where(jnp.logical_or(i == 1, i == 2), 1, 0)

    def send_step(i, carry):
        x_, h = order_step(i)
        core_out[x_ * 2 + h] = down(x_, 1 - c, h).astype(BF16)
        for j in range(NZ):
            for y_ in (1 - y, y):
                core_copy(x_, h, dest_at(j), y_).start()
        return carry

    lax.fori_loop(0, 4, send_step, 0)

    def keep_step(i, carry):
        x_, h = order_step(i)
        part[x_ * 2 + h] = down(x_, c, h)
        return carry

    lax.fori_loop(0, 4, keep_step, 0)

    def chip_sum(h, x_, z_, y_):
        i = x_ * 2 + h
        return part[i, row_at(z_, y_), :] + core_in[i, row_at(z_, y_), :].astype(F32)

    def first_slot(h, other, z_):
        return h * 2 * NZ + (NZ if other else 0) + z_

    def first_copy(h, other, z_):
        i = first_slot(h, other, z_)
        return remote(
            first_out.at[i], first_in.at[i], sem_f_s.at[i], sem_f_r.at[i],
            x_peer if h == 0 else y_peer,
        )

    def second_copy(h, z_):
        i = h * NZ + z_
        return remote(
            second_out.at[i], second_in.at[i], sem_s_s.at[i], sem_s_r.at[i],
            y_peer if h == 0 else x_peer,
        )

    zs = range(NZ)

    def first_send(z_):
        for other in (True, False):
            y_ = 1 - y if other else y
            core_copy(1 - x, 0, z_, y_).wait_recv()
            first_out[first_slot(0, other, z_)] = chip_sum(0, 1 - x, z_, y_).astype(BF16)
            first_copy(0, other, z_).start()
            x_ = 1 - x if other else x
            core_copy(x_, 1, z_, 1 - y).wait_recv()
            first_out[first_slot(1, other, z_)] = chip_sum(1, x_, z_, 1 - y).astype(BF16)
            first_copy(1, other, z_).start()

    def second_send(z_):
        for h in range(2):
            x_, y_ = (x, 1 - y) if h == 0 else (1 - x, y)
            core_copy(x_, h, z_, y_).wait_recv()
            first_copy(h, True, z_).wait_recv()
            second_out[h * NZ + z_] = (
                chip_sum(h, x_, z_, y_) + first_in[first_slot(h, True, z_)].astype(F32)
            ).astype(BF16)
            second_copy(h, z_).start()

    def gather_total(z_):
        for h in range(2):
            core_copy(x, h, z_, y).wait_recv()
            first_copy(h, False, z_).wait_recv()
            second_copy(h, z_).wait_recv()
            total[h * NZ + z_] = (
                chip_sum(h, x, z_, y)
                + first_in[first_slot(h, False, z_)].astype(F32)
                + second_in[h * NZ + z_].astype(F32)
            )

    def line_copy(h, up, dest):
        i = h * 2 * NZ + up * NZ + dest
        return remote(
            line_out.at[i], line_in.at[i], sem_l_s.at[i], sem_l_r.at[i],
            dev(x, jnp.where(up == 1, z + 1, z - 1), y, c),
        )

    def line_send(j, relayed):
        dest = dest_at(j)
        up = jnp.where(dest > z, 1, 0)
        feeds = jnp.where(up == 1, z, NZ - 1 - z) > 0

        @pl.when(feeds if relayed else jnp.logical_not(feeds))
        def _():
            for h in range(2):
                i = h * 2 * NZ + up * NZ + dest
                if relayed:
                    line_copy(h, up, dest).wait_recv()
                    line_out[i] = (total[h * NZ + dest] + line_in[i].astype(F32)).astype(BF16)
                else:
                    line_out[i] = total[h * NZ + dest].astype(BF16)
                line_copy(h, up, dest).start()

    for turn in range(NZ + 3):
        if turn < NZ:
            first_send(dest_at(turn))
        if 0 <= turn - 1 < NZ:
            second_send(dest_at(turn - 1))
        if 0 <= turn - 2 < NZ:
            gather_total(dest_at(turn - 2))
        if 0 <= turn - 2 < NZ - 1:
            line_send(turn - 2, False)
        if 0 <= turn - 3 < NZ - 1:
            line_send(turn - 3, True)

    for h in range(2):
        for up in range(2):
            @pl.when((z > 0) if up == 1 else (z < NZ - 1))
            def _():
                line_copy(h, up, z).wait_recv()
                total[h * NZ + z] += line_in[h * 2 * NZ + up * NZ + z].astype(F32)

    fin_copy = remote(fin_out, fin_in, sem_fin.at[0], sem_fin.at[1], sibling)
    halves = []
    for h in range(2):
        whole = total[h * NZ + z]
        lower, upper = whole[:count], whole[count:]
        fin_out[h] = jnp.where(c == 0, upper, lower).astype(BF16)
        halves.append(jnp.where(c == 0, lower, upper).astype(BF16))
    fin_copy.start()
    fin_copy.wait()
    for h in range(2):
        theirs = fin_in[h].astype(F32)
        mine = halves[h].astype(F32)
        out_ref[:, h * chunk:(h + 1) * chunk] = jnp.where(c == 0, mine, theirs).astype(BF16)
        out_ref[:, (2 + h) * chunk:(3 + h) * chunk] = jnp.where(c == 0, theirs, mine).astype(BF16)

    for step in range(1, N_DEV):
        remote(
            table.at[me], table.at[me], sem_tab_s.at[step], sem_tab_r.at[me], sibling
        ).wait_send()
    for h in range(2):
        for k in range(NZ):
            def sent(z_, up):
                if up is None or up:
                    @pl.when(z < NZ - 1)
                    def _():
                        along_line(h, z_, True).wait_send()
                if not up:
                    @pl.when(z > 0)
                    def _():
                        along_line(h, z_, False).wait_send()

            level(k, sent)
        for z_ in zs:
            first_hop(h, z_).wait_send()
            second_hop(h, z_, True).wait_send()
            second_hop(h, z_, False).wait_send()
            for x_ in range(2):
                for y_ in range(2):
                    @pl.when(jnp.logical_or(x_ != x, jnp.logical_or(z_ != z, y_ != y)))
                    def _():
                        to_sibling(h, x_, z_, y_).wait_send()
            first_copy(h, True, z_).wait_send()
            first_copy(h, False, z_).wait_send()
            second_copy(h, z_).wait_send()
        for x_ in range(2):
            for z_ in zs:
                for y_ in range(2):
                    core_copy(x_, h, z_, y_).wait_send()
    for j in range(NZ - 1):
        dest = dest_at(j)
        for h in range(2):
            line_copy(h, jnp.where(dest > z, 1, 0), dest).wait_send()


def fused(tokens, expert_ids, gate_weights, w_gate, w_up, w_down):
    count, share = tokens.shape
    hid, width = w_gate.shape[1:]
    chunk = share // 4
    block = 2 * count
    n_rows = N_PAIR * block
    dma = pltpu.SemaphoreType.DMA
    vmem = lambda shape, dtype: pltpu.VMEM(shape, dtype)
    blocks = lambda n: pltpu.VMEM((n, block, chunk), BF16)
    return pl.pallas_call(
        moe_kernel,
        out_shape=jax.ShapeDtypeStruct((count, share), BF16),
        in_specs=[pl.BlockSpec(memory_space=pltpu.VMEM)] * 3 + [pl.BlockSpec(memory_space=pl.ANY)] * 3,
        out_specs=pl.BlockSpec(memory_space=pltpu.VMEM),
        scratch_shapes=[
            vmem((hid, width), BF16), vmem((hid, width), BF16), vmem((hid, width), BF16),
            vmem((8, n_rows, chunk), BF16), vmem((count, share), BF16),
            vmem((N_DEV, count, 128), F32),
            vmem((n_rows, hid), F32), vmem((n_rows, hid), F32), vmem((n_rows, hid), BF16),
            vmem((n_rows, 128), F32),
            vmem((4, n_rows, chunk), F32), vmem((4, n_rows, chunk), BF16), vmem((4, n_rows, chunk), BF16),
            blocks(4 * NZ), blocks(4 * NZ), blocks(2 * NZ), blocks(2 * NZ),
            vmem((2 * NZ, block, chunk), F32), blocks(4 * NZ), blocks(4 * NZ),
            vmem((2, count, chunk), BF16), vmem((2, count, chunk), BF16),
            dma((3,)), dma((2,)), dma((N_DEV,)), dma((N_DEV,)),
            dma((4 * NZ,)), dma((2 * NZ,)), dma((2 * NZ,)), dma((2 * NZ,)),
            dma((4 * NZ,)), dma((4 * NZ,)), dma((8 * NZ,)), dma((8 * NZ,)),
            dma((8 * NZ,)), dma((8 * NZ,)), dma((4 * NZ,)), dma((4 * NZ,)), dma((2 * NZ,)), dma((2 * NZ,)),
            dma((4 * NZ,)), dma((4 * NZ,)), dma((2,)),
        ],
        compiler_params=pltpu.CompilerParams(
            collective_id=0, has_side_effects=True, vmem_limit_bytes=60 * 1024 * 1024
        ),
        cost_estimate=pl.CostEstimate(
            flops=6 * n_rows * hid * width, bytes_accessed=6 * hid * width,
            transcendentals=n_rows * hid,
        ),
    )(tokens, expert_ids, gate_weights, w_gate, w_up, w_down)


def on_device(tokens, expert_ids, gate_weights, w_gate, w_up, w_down):
    n_dest = lax.axis_size("expert")
    token_count = tokens.shape[0]
    chosen = expert_ids.shape[1]
    width = w_gate.shape[2]
    capacity = min(token_count, token_count * chosen * 4 // (3 * n_dest))
    flat_ids = expert_ids.reshape(-1)
    onehot = (flat_ids[:, None] == jnp.arange(n_dest, dtype=jnp.int32)[None, :]).astype(jnp.int32)
    order_rank = jnp.cumsum(onehot, axis=0) - 1
    slot_index = jnp.sum(order_rank * onehot, axis=1)
    target = flat_ids * capacity + slot_index
    token_of = jnp.arange(token_count * chosen, dtype=jnp.int32) // chosen
    matches = (jnp.arange(n_dest * capacity, dtype=jnp.int32)[:, None] == target[None, :]).astype(
        jnp.bfloat16
    )
    token_map = (token_of[:, None] == jnp.arange(token_count, dtype=jnp.int32)[None, :]).astype(
        jnp.bfloat16
    )
    dispatch_matrix = jnp.dot(matches, token_map, preferred_element_type=jnp.float32).astype(
        jnp.bfloat16
    )
    scaled_map = token_map * gate_weights.reshape(-1)[:, None]
    combine_matrix = jnp.dot(scaled_map.T, matches.T, preferred_element_type=jnp.float32).astype(
        jnp.bfloat16
    )
    contract_last = (((1,), (1,)), ((), ()))
    features = lax.all_gather(tokens, "section", axis=1, tiled=True)
    send_rows = jnp.dot(dispatch_matrix, features, preferred_element_type=jnp.float32).astype(
        jnp.bfloat16
    )
    send_rows = send_rows.reshape(n_dest, capacity, width)
    received = lax.all_to_all(send_rows, "expert", split_axis=0, concat_axis=0, tiled=True)
    inputs = received.reshape(-1, width)
    gated = lax.dot_general(inputs, w_gate[0], contract_last, preferred_element_type=jnp.float32)
    upward = lax.dot_general(inputs, w_up[0], contract_last, preferred_element_type=jnp.float32)
    hidden = (jax.nn.silu(gated) * upward).astype(jnp.bfloat16)
    partial_value = jnp.dot(hidden, w_down[0], preferred_element_type=jnp.float32).astype(
        jnp.bfloat16
    )
    partial_value = partial_value.reshape((received.shape[0], received.shape[1], width))
    returned = lax.all_to_all(partial_value, "expert", split_axis=0, concat_axis=0, tiled=True)
    weighted = jnp.dot(
        combine_matrix, returned.reshape(-1, width), preferred_element_type=jnp.float32
    )
    return lax.psum_scatter(weighted, "section", scatter_dimension=1, tiled=True).astype(
        jnp.bfloat16
    )


def solution(mesh):
    placed = (
        P("expert", "section"),
        P("expert", None),
        P("expert", None),
        P("expert", "section", None),
        P("expert", "section", None),
        P("expert", "section", None),
    )
    whole_kernel = mesh.shape["section"] == 2 and mesh.shape["expert"] == N_DEV
    return jax.shard_map(
        fused if whole_kernel else on_device, mesh=mesh, in_specs=placed, out_specs=P("expert", "section"), check_vma=False
    )
```

```python
import functools
import jax
import jax.numpy as jnp
from jax import lax
from jax.experimental import pallas as pl
from jax.experimental.pallas import tpu as pltpu
from jax.sharding import PartitionSpec as P

MESH = pl.DeviceIdType.MESH
F32 = jnp.float32
BF16 = jnp.bfloat16
NZ = 4
N_PAIR = 2 * NZ
N_DEV = 2 * N_PAIR


def moe_kernel(
    tok_ref, ids_ref, gw_ref, wg_hbm, wu_hbm, wd_hbm, out_ref,
    wg, wu, wd, rows_x, tok_sib, table, gated, upward, hidden, scale,
    part, core_out, core_in, first_out, first_in, second_out, second_in,
    total, line_out, line_in, fin_out, fin_in,
    sem_w, sem_tok, sem_tab_s, sem_tab_r,
    sem_line_s, sem_line_r, sem_d1_s, sem_d1_r, sem_d2_s, sem_d2_r, sem_core_s, sem_core_r,
    sem_cx_s, sem_cx_r, sem_f_s, sem_f_r, sem_s_s, sem_s_r, sem_l_s, sem_l_r, sem_fin,
):
    count, _ = tok_ref.shape
    block = 2 * count
    chunk = rows_x.shape[2]
    me = lax.axis_index("expert")
    x = lax.axis_index("section")
    z, y, c = me // 4, (me // 2) % 2, me % 2

    def dev(x_, z_, y_, c_):
        return {"section": x_, "expert": z_ * 4 + y_ * 2 + c_}

    sibling = dev(x, z, y, 1 - c)
    x_peer = dev(1 - x, z, y, c)
    y_peer = dev(x, z, 1 - y, c)

    def remote(src, dst, s, r, to):
        return pltpu.make_async_remote_copy(
            src_ref=src, dst_ref=dst, send_sem=s, recv_sem=r, device_id=to, device_id_type=MESH
        )

    def row_at(z_, y_):
        return pl.ds(pl.multiple_of((y_ * NZ + z_) * block, block), block)

    weight_copies = [
        pltpu.make_async_copy(wg_hbm.at[0], wg, sem_w.at[0]),
        pltpu.make_async_copy(wu_hbm.at[0], wu, sem_w.at[1]),
        pltpu.make_async_copy(wd_hbm.at[0], wd, sem_w.at[2]),
    ]
    for copy in weight_copies:
        copy.start()

    barrier = pltpu.get_barrier_semaphore()
    for step in range(1, N_DEV):
        pl.semaphore_signal(
            barrier, inc=1, device_id={"section": x, "expert": (me + step) % N_DEV},
            device_id_type=MESH,
        )
    pl.semaphore_signal(barrier, inc=1, device_id=x_peer, device_id_type=MESH)
    pl.semaphore_wait(barrier, N_DEV)

    tok_copy = remote(tok_ref, tok_sib, sem_tok.at[0], sem_tok.at[1], sibling)
    tok_copy.start()

    lane = lax.broadcasted_iota(jnp.int32, (count, 128), 1)
    weights = jnp.zeros((count, 128), F32)
    ids = jnp.transpose(ids_ref[...])
    gains = jnp.transpose(gw_ref[...].astype(F32))
    for k in range(ids_ref.shape[0]):
        weights = weights + jnp.where(lane == ids[:, k:k + 1], gains[:, k:k + 1], 0.0)
    table[me] = weights

    tok_copy.wait()
    for j in range(4):
        cols = slice(j * chunk, (j + 1) * chunk)
        mine, other = tok_ref[:, cols], tok_sib[:, cols]
        lower = jnp.where(c == 0, mine.astype(F32), other.astype(F32)).astype(BF16)
        upper = jnp.where(c == 0, other.astype(F32), mine.astype(F32)).astype(BF16)
        rows_x[x * 4 + j, row_at(z, y), :] = (
            jnp.concatenate([lower, upper], axis=0)
        )

    def spot(h, x_, z_, y_):
        return rows_x.at[
            x_ * 4 + c * 2 + h, row_at(z_, y_), :
        ]

    def label(h, x_, z_, y_):
        return h * 4 * NZ + x_ * N_PAIR + z_ * 2 + y_

    def along_line(h, z_, up):
        place = spot(h, x, z_, y)
        to = dev(x, z + 1 if up else z - 1, y, c)
        return remote(
            place, place, sem_line_s.at[h * 2 * NZ + (0 if up else NZ) + z_],
            sem_line_r.at[h * NZ + z_], to,
        )

    def first_hop(h, z_):
        place = spot(h, x, z_, y)
        return remote(
            place, place, sem_d1_s.at[h * NZ + z_], sem_d1_r.at[h * NZ + z_],
            y_peer if h == 0 else x_peer,
        )

    def first_arrived(h, z_):
        return (h, x, z_, 1 - y) if h == 0 else (h, 1 - x, z_, y)

    def first_wait(h, z_):
        place = spot(*first_arrived(h, z_))
        remote(place, place, sem_d1_s.at[h * NZ + z_], sem_d1_r.at[h * NZ + z_], sibling).wait_recv()

    def second_hop(h, z_, own):
        place = spot(h, x, z_, y) if own else spot(*first_arrived(h, z_))
        i = h * 2 * NZ + (0 if own else NZ) + z_
        return remote(
            place, place, sem_d2_s.at[i], sem_d2_r.at[i], x_peer if h == 0 else y_peer
        )

    def second_arrived(h, z_, own):
        if h == 0:
            return (h, 1 - x, z_, y if own else 1 - y)
        return (h, x if own else 1 - x, z_, 1 - y)

    def second_wait(h, z_, own):
        place = spot(*second_arrived(h, z_, own))
        i = h * 2 * NZ + (0 if own else NZ) + z_
        remote(place, place, sem_d2_s.at[i], sem_d2_r.at[i], sibling).wait_recv()

    def to_sibling(h, x_, z_, y_):
        place = spot(h, x_, z_, y_)
        i = label(h, x_, z_, y_)
        return remote(place, place, sem_core_s.at[i], sem_core_r.at[i], sibling)

    def from_sibling(h, x_, z_, y_):
        place = rows_x.at[
            x_ * 4 + (1 - c) * 2 + h, row_at(z_, y_), :
        ]
        i = label(h, x_, z_, y_)
        return remote(place, place, sem_core_s.at[i], sem_core_r.at[i], sibling)

    def level(k, fn):
        if k == 0:
            fn(z, None)
            return

        @pl.when(z - k >= 0)
        def _():
            fn(z - k, True)

        @pl.when(z + k < NZ)
        def _():
            fn(z + k, False)

    for h in range(2):
        @pl.when(z < NZ - 1)
        def _():
            along_line(h, z, True).start()

        @pl.when(z > 0)
        def _():
            along_line(h, z, False).start()

        first_hop(h, z).start()
        second_hop(h, z, True).start()

    for step in range(1, N_DEV):
        peer = (me + step) % N_DEV
        remote(
            table.at[me], table.at[me], sem_tab_s.at[step], sem_tab_r.at[me],
            {"section": x, "expert": peer},
        ).start()

    for k in range(1, NZ + 1):
        for h in range(2):
            if k < NZ:
                def arrived(z_, up):
                    place = spot(h, x, z_, y)
                    remote(
                        place, place, sem_line_s.at[h * 2 * NZ + z_], sem_line_r.at[h * NZ + z_],
                        sibling,
                    ).wait_recv()
                    if up:
                        @pl.when(z < NZ - 1)
                        def _():
                            along_line(h, z_, True).start()
                    else:
                        @pl.when(z > 0)
                        def _():
                            along_line(h, z_, False).start()
                    first_hop(h, z_).start()
                    second_hop(h, z_, True).start()
                    to_sibling(h, x, z_, y).start()

                level(k, arrived)
        for h in range(2):
            def arrived_first(z_, up):
                first_wait(h, z_)
                second_hop(h, z_, False).start()
                to_sibling(*first_arrived(h, z_)).start()

            level(k - 1, arrived_first)

    contract_last = (((1,), (1,)), ((), ()))
    gated[...] = jnp.zeros_like(gated)
    upward[...] = jnp.zeros_like(upward)
    weight_copies[0].wait()
    weight_copies[1].wait()
    half_rows = NZ * block

    def up_add(q, where):
        cols = pl.ds(pl.multiple_of(q * chunk, 128), chunk)
        inputs = rows_x[q, where, :]
        gated[where, :] += lax.dot_general(inputs, wg[:, cols], contract_last, preferred_element_type=F32)
        upward[where, :] += lax.dot_general(inputs, wu[:, cols], contract_last, preferred_element_type=F32)

    def up_all_rows(x_):
        def body(i, carry):
            up_add(x_ * 4 + i * 2, pl.ds(0, 2 * half_rows))
            return carry

        lax.fori_loop(0, 2, body, 0)

    def up_half_rows(y_):
        def body(i, carry):
            up_add(i * 2 + 1, pl.ds(pl.multiple_of(y_ * half_rows, half_rows), half_rows))
            return carry

        lax.fori_loop(0, 4, body, 0)

    def wait_sibling(h, x_, y_):
        for z_ in range(NZ):
            @pl.when(jnp.logical_or(x_ != x, jnp.logical_or(z_ != z, y_ != y)))
            def _():
                from_sibling(h, x_, z_, y_).wait_recv()

    def drain(items):
        for own, k in items:
            for h in range(2):
                def arrived_second(z_, up):
                    second_wait(h, z_, own)
                    to_sibling(*second_arrived(h, z_, own)).start()

                level(k, arrived_second)

    for y_ in (y, 1 - y):
        wait_sibling(0, x, y_)
    up_all_rows(x)
    drain(((True, 0), (True, 1), (False, 0), (True, 2)))
    for x_ in (x, 1 - x):
        wait_sibling(1, x_, y)
    up_half_rows(y)
    drain(((False, 1), (True, 3), (False, 2), (False, 3)))
    for y_ in (y, 1 - y):
        wait_sibling(0, 1 - x, y_)
    up_all_rows(1 - x)
    for x_ in (x, 1 - x):
        wait_sibling(1, x_, 1 - y)
    up_half_rows(1 - y)
    value = gated[...]
    hidden[...] = (value / (1.0 + jnp.exp(-value)) * upward[...]).astype(BF16)

    for step in range(1, N_DEV):
        peer = (me + N_DEV - step) % N_DEV
        remote(
            table.at[peer], table.at[peer], sem_tab_s.at[step], sem_tab_r.at[peer], sibling
        ).wait_recv()
    lane = lax.broadcasted_iota(jnp.int32, (N_DEV * count, 128), 1)
    every = jnp.concatenate([table[z_ * 4 + y_ * 2 + c_] for y_ in range(2) for z_ in range(NZ) for c_ in range(2)], axis=0)
    scale[...] = jnp.broadcast_to(
        jnp.sum(jnp.where(lane == me, every, 0.0), axis=1, keepdims=True), scale.shape
    )

    weight_copies[2].wait()
    n_rows = N_PAIR * block

    def down(x_, c_, h):
        q = x_ * 4 + c_ * 2 + h
        cols = pl.ds(pl.multiple_of(q * chunk, 128), chunk)
        return jnp.dot(hidden[...], wd[:, cols], preferred_element_type=F32) * scale[:, 0:1]

    def dest_at(j):
        a, b, d, e = ((3, 3, 0, 0), (2, 0, 3, 1), (1, 2, 1, 2), (0, 1, 2, 3))[j]
        return jnp.where(z == 0, a, jnp.where(z == 1, b, jnp.where(z == 2, d, e)))

    def core_copy(x_, h, z_, y_):
        i = x_ * 2 + h
        n = i * N_PAIR + z_ * 2 + y_
        return remote(
            core_out.at[i, row_at(z_, y_), :], core_in.at[i, row_at(z_, y_), :],
            sem_cx_s.at[n], sem_cx_r.at[n], sibling,
        )

    def order_step(i):
        return jnp.where(i < 2, 1 - x, x), jnp.where(jnp.logical_or(i == 1, i == 2), 1, 0)

    def send_step(i, carry):
        x_, h = order_step(i)
        core_out[x_ * 2 + h] = down(x_, 1 - c, h).astype(BF16)
        for j in range(NZ):
            for y_ in (1 - y, y):
                core_copy(x_, h, dest_at(j), y_).start()
        return carry

    lax.fori_loop(0, 4, send_step, 0)

    def keep_step(i, carry):
        x_, h = order_step(i)
        part[x_ * 2 + h] = down(x_, c, h)
        return carry

    lax.fori_loop(0, 4, keep_step, 0)

    def chip_sum(h, x_, z_, y_):
        i = x_ * 2 + h
        return part[i, row_at(z_, y_), :] + core_in[i, row_at(z_, y_), :].astype(F32)

    def first_slot(h, other, z_):
        return h * 2 * NZ + (NZ if other else 0) + z_

    def first_copy(h, other, z_):
        i = first_slot(h, other, z_)
        return remote(
            first_out.at[i], first_in.at[i], sem_f_s.at[i], sem_f_r.at[i],
            x_peer if h == 0 else y_peer,
        )

    def second_copy(h, z_):
        i = h * NZ + z_
        return remote(
            second_out.at[i], second_in.at[i], sem_s_s.at[i], sem_s_r.at[i],
            y_peer if h == 0 else x_peer,
        )

    zs = range(NZ)

    def first_send(z_):
        for other in (True, False):
            y_ = 1 - y if other else y
            core_copy(1 - x, 0, z_, y_).wait_recv()
            first_out[first_slot(0, other, z_)] = chip_sum(0, 1 - x, z_, y_).astype(BF16)
            first_copy(0, other, z_).start()
            x_ = 1 - x if other else x
            core_copy(x_, 1, z_, 1 - y).wait_recv()
            first_out[first_slot(1, other, z_)] = chip_sum(1, x_, z_, 1 - y).astype(BF16)
            first_copy(1, other, z_).start()

    def second_send(z_):
        for h in range(2):
            x_, y_ = (x, 1 - y) if h == 0 else (1 - x, y)
            core_copy(x_, h, z_, y_).wait_recv()
            first_copy(h, True, z_).wait_recv()
            second_out[h * NZ + z_] = (
                chip_sum(h, x_, z_, y_) + first_in[first_slot(h, True, z_)].astype(F32)
            ).astype(BF16)
            second_copy(h, z_).start()

    def gather_total(z_):
        for h in range(2):
            core_copy(x, h, z_, y).wait_recv()
            first_copy(h, False, z_).wait_recv()
            second_copy(h, z_).wait_recv()
            total[h * NZ + z_] = (
                chip_sum(h, x, z_, y)
                + first_in[first_slot(h, False, z_)].astype(F32)
                + second_in[h * NZ + z_].astype(F32)
            )

    def line_copy(h, up, dest):
        i = h * 2 * NZ + up * NZ + dest
        return remote(
            line_out.at[i], line_in.at[i], sem_l_s.at[i], sem_l_r.at[i],
            dev(x, jnp.where(up == 1, z + 1, z - 1), y, c),
        )

    def line_send(j, relayed):
        dest = dest_at(j)
        up = jnp.where(dest > z, 1, 0)
        feeds = jnp.where(up == 1, z, NZ - 1 - z) > 0

        @pl.when(feeds if relayed else jnp.logical_not(feeds))
        def _():
            for h in range(2):
                i = h * 2 * NZ + up * NZ + dest
                if relayed:
                    line_copy(h, up, dest).wait_recv()
                    line_out[i] = (total[h * NZ + dest] + line_in[i].astype(F32)).astype(BF16)
                else:
                    line_out[i] = total[h * NZ + dest].astype(BF16)
                line_copy(h, up, dest).start()

    for turn in range(NZ + 3):
        if turn < NZ:
            first_send(dest_at(turn))
        if 0 <= turn - 1 < NZ:
            second_send(dest_at(turn - 1))
        if 0 <= turn - 2 < NZ:
            gather_total(dest_at(turn - 2))
        if 0 <= turn - 2 < NZ - 1:
            line_send(turn - 2, False)
        if 0 <= turn - 3 < NZ - 1:
            line_send(turn - 3, True)

    for h in range(2):
        for up in range(2):
            @pl.when((z > 0) if up == 1 else (z < NZ - 1))
            def _():
                line_copy(h, up, z).wait_recv()
                total[h * NZ + z] += line_in[h * 2 * NZ + up * NZ + z].astype(F32)

    fin_copy = remote(fin_out, fin_in, sem_fin.at[0], sem_fin.at[1], sibling)
    halves = []
    for h in range(2):
        whole = total[h * NZ + z]
        lower, upper = whole[:count], whole[count:]
        fin_out[h] = jnp.where(c == 0, upper, lower).astype(BF16)
        halves.append(jnp.where(c == 0, lower, upper).astype(BF16))
    fin_copy.start()
    fin_copy.wait()
    for h in range(2):
        theirs = fin_in[h].astype(F32)
        mine = halves[h].astype(F32)
        out_ref[:, h * chunk:(h + 1) * chunk] = jnp.where(c == 0, mine, theirs).astype(BF16)
        out_ref[:, (2 + h) * chunk:(3 + h) * chunk] = jnp.where(c == 0, theirs, mine).astype(BF16)

    for step in range(1, N_DEV):
        remote(
            table.at[me], table.at[me], sem_tab_s.at[step], sem_tab_r.at[me], sibling
        ).wait_send()
    for h in range(2):
        for k in range(NZ):
            def sent(z_, up):
                if up is None or up:
                    @pl.when(z < NZ - 1)
                    def _():
                        along_line(h, z_, True).wait_send()
                if not up:
                    @pl.when(z > 0)
                    def _():
                        along_line(h, z_, False).wait_send()

            level(k, sent)
        for z_ in zs:
            first_hop(h, z_).wait_send()
            second_hop(h, z_, True).wait_send()
            second_hop(h, z_, False).wait_send()
            for x_ in range(2):
                for y_ in range(2):
                    @pl.when(jnp.logical_or(x_ != x, jnp.logical_or(z_ != z, y_ != y)))
                    def _():
                        to_sibling(h, x_, z_, y_).wait_send()
            first_copy(h, True, z_).wait_send()
            first_copy(h, False, z_).wait_send()
            second_copy(h, z_).wait_send()
        for x_ in range(2):
            for z_ in zs:
                for y_ in range(2):
                    core_copy(x_, h, z_, y_).wait_send()
    for j in range(NZ - 1):
        dest = dest_at(j)
        for h in range(2):
            line_copy(h, jnp.where(dest > z, 1, 0), dest).wait_send()


def fused(tokens, expert_ids, gate_weights, w_gate, w_up, w_down):
    count, share = tokens.shape
    hid, width = w_gate.shape[1:]
    chunk = share // 4
    block = 2 * count
    n_rows = N_PAIR * block
    dma = pltpu.SemaphoreType.DMA
    vmem = lambda shape, dtype: pltpu.VMEM(shape, dtype)
    blocks = lambda n: pltpu.VMEM((n, block, chunk), BF16)
    return pl.pallas_call(
        moe_kernel,
        out_shape=jax.ShapeDtypeStruct((count, share), BF16),
        in_specs=[pl.BlockSpec(memory_space=pltpu.VMEM)] * 3 + [pl.BlockSpec(memory_space=pl.ANY)] * 3,
        out_specs=pl.BlockSpec(memory_space=pltpu.VMEM),
        scratch_shapes=[
            vmem((hid, width), BF16), vmem((hid, width), BF16), vmem((hid, width), BF16),
            vmem((8, n_rows, chunk), BF16), vmem((count, share), BF16),
            vmem((N_DEV, count, 128), F32),
            vmem((n_rows, hid), F32), vmem((n_rows, hid), F32), vmem((n_rows, hid), BF16),
            vmem((n_rows, 128), F32),
            vmem((4, n_rows, chunk), F32), vmem((4, n_rows, chunk), BF16), vmem((4, n_rows, chunk), BF16),
            blocks(4 * NZ), blocks(4 * NZ), blocks(2 * NZ), blocks(2 * NZ),
            vmem((2 * NZ, block, chunk), F32), blocks(4 * NZ), blocks(4 * NZ),
            vmem((2, count, chunk), BF16), vmem((2, count, chunk), BF16),
            dma((3,)), dma((2,)), dma((N_DEV,)), dma((N_DEV,)),
            dma((4 * NZ,)), dma((2 * NZ,)), dma((2 * NZ,)), dma((2 * NZ,)),
            dma((4 * NZ,)), dma((4 * NZ,)), dma((8 * NZ,)), dma((8 * NZ,)),
            dma((8 * NZ,)), dma((8 * NZ,)), dma((4 * NZ,)), dma((4 * NZ,)), dma((2 * NZ,)), dma((2 * NZ,)),
            dma((4 * NZ,)), dma((4 * NZ,)), dma((2,)),
        ],
        compiler_params=pltpu.CompilerParams(
            collective_id=0, has_side_effects=True, vmem_limit_bytes=60 * 1024 * 1024
        ),
        cost_estimate=pl.CostEstimate(
            flops=6 * n_rows * hid * width, bytes_accessed=6 * hid * width,
            transcendentals=n_rows * hid,
        ),
    )(tokens, expert_ids.T, gate_weights.T, w_gate, w_up, w_down)


def on_device(tokens, expert_ids, gate_weights, w_gate, w_up, w_down):
    n_dest = lax.axis_size("expert")
    token_count = tokens.shape[0]
    chosen = expert_ids.shape[1]
    width = w_gate.shape[2]
    capacity = min(token_count, token_count * chosen * 4 // (3 * n_dest))
    flat_ids = expert_ids.reshape(-1)
    onehot = (flat_ids[:, None] == jnp.arange(n_dest, dtype=jnp.int32)[None, :]).astype(jnp.int32)
    order_rank = jnp.cumsum(onehot, axis=0) - 1
    slot_index = jnp.sum(order_rank * onehot, axis=1)
    target = flat_ids * capacity + slot_index
    token_of = jnp.arange(token_count * chosen, dtype=jnp.int32) // chosen
    matches = (jnp.arange(n_dest * capacity, dtype=jnp.int32)[:, None] == target[None, :]).astype(
        jnp.bfloat16
    )
    token_map = (token_of[:, None] == jnp.arange(token_count, dtype=jnp.int32)[None, :]).astype(
        jnp.bfloat16
    )
    dispatch_matrix = jnp.dot(matches, token_map, preferred_element_type=jnp.float32).astype(
        jnp.bfloat16
    )
    scaled_map = token_map * gate_weights.reshape(-1)[:, None]
    combine_matrix = jnp.dot(scaled_map.T, matches.T, preferred_element_type=jnp.float32).astype(
        jnp.bfloat16
    )
    contract_last = (((1,), (1,)), ((), ()))
    features = lax.all_gather(tokens, "section", axis=1, tiled=True)
    send_rows = jnp.dot(dispatch_matrix, features, preferred_element_type=jnp.float32).astype(
        jnp.bfloat16
    )
    send_rows = send_rows.reshape(n_dest, capacity, width)
    received = lax.all_to_all(send_rows, "expert", split_axis=0, concat_axis=0, tiled=True)
    inputs = received.reshape(-1, width)
    gated = lax.dot_general(inputs, w_gate[0], contract_last, preferred_element_type=jnp.float32)
    upward = lax.dot_general(inputs, w_up[0], contract_last, preferred_element_type=jnp.float32)
    hidden = (jax.nn.silu(gated) * upward).astype(jnp.bfloat16)
    partial_value = jnp.dot(hidden, w_down[0], preferred_element_type=jnp.float32).astype(
        jnp.bfloat16
    )
    partial_value = partial_value.reshape((received.shape[0], received.shape[1], width))
    returned = lax.all_to_all(partial_value, "expert", split_axis=0, concat_axis=0, tiled=True)
    weighted = jnp.dot(
        combine_matrix, returned.reshape(-1, width), preferred_element_type=jnp.float32
    )
    return lax.psum_scatter(weighted, "section", scatter_dimension=1, tiled=True).astype(
        jnp.bfloat16
    )


def solution(mesh):
    placed = (
        P("expert", "section"),
        P("expert", None),
        P("expert", None),
        P("expert", "section", None),
        P("expert", "section", None),
        P("expert", "section", None),
    )
    whole_kernel = mesh.shape["section"] == 2 and mesh.shape["expert"] == N_DEV
    return jax.shard_map(
        fused if whole_kernel else on_device, mesh=mesh, in_specs=placed, out_specs=P("expert", "section"), check_vma=False
    )
```

```python
import functools
import jax
import jax.numpy as jnp
from jax import lax
from jax.experimental import pallas as pl
from jax.experimental.pallas import tpu as pltpu
from jax.sharding import PartitionSpec as P

MESH = pl.DeviceIdType.MESH
F32 = jnp.float32
BF16 = jnp.bfloat16
NZ = 4
N_PAIR = 2 * NZ
N_DEV = 2 * N_PAIR


def moe_kernel(
    tok_ref, ids_ref, gw_ref, wg_hbm, wu_hbm, wd_hbm, out_ref,
    wg, wu, wd, rows_x, tok_sib, table, gated, upward, hidden, scale,
    part, core_out, core_in, first_out, first_in, second_out, second_in,
    total, line_out, line_in, fin_out, fin_in,
    sem_w, sem_tok, sem_tab_s, sem_tab_r,
    sem_line_s, sem_line_r, sem_d1_s, sem_d1_r, sem_d2_s, sem_d2_r, sem_core_s, sem_core_r,
    sem_cx_s, sem_cx_r, sem_f_s, sem_f_r, sem_s_s, sem_s_r, sem_l_s, sem_l_r, sem_fin,
):
    count, _ = tok_ref.shape
    block = 2 * count
    chunk = rows_x.shape[2]
    me = lax.axis_index("expert")
    x = lax.axis_index("section")
    z, y, c = me // 4, (me // 2) % 2, me % 2

    def dev(x_, z_, y_, c_):
        return {"section": x_, "expert": z_ * 4 + y_ * 2 + c_}

    sibling = dev(x, z, y, 1 - c)
    x_peer = dev(1 - x, z, y, c)
    y_peer = dev(x, z, 1 - y, c)

    def remote(src, dst, s, r, to):
        return pltpu.make_async_remote_copy(
            src_ref=src, dst_ref=dst, send_sem=s, recv_sem=r, device_id=to, device_id_type=MESH
        )

    def row_at(z_, y_):
        return pl.ds(pl.multiple_of((y_ * NZ + z_) * block, block), block)

    weight_copies = [
        pltpu.make_async_copy(wg_hbm.at[0], wg, sem_w.at[0]),
        pltpu.make_async_copy(wu_hbm.at[0], wu, sem_w.at[1]),
        pltpu.make_async_copy(wd_hbm.at[0], wd, sem_w.at[2]),
    ]
    for copy in weight_copies:
        copy.start()

    barrier = pltpu.get_barrier_semaphore()
    for step in range(1, N_DEV):
        pl.semaphore_signal(
            barrier, inc=1, device_id={"section": x, "expert": (me + step) % N_DEV},
            device_id_type=MESH,
        )
    pl.semaphore_signal(barrier, inc=1, device_id=x_peer, device_id_type=MESH)

    lane = lax.broadcasted_iota(jnp.int32, (count, 128), 1)
    weights = jnp.zeros((count, 128), F32)
    ids = jnp.transpose(ids_ref[...])
    gains = jnp.transpose(gw_ref[...].astype(F32))
    for k in range(ids_ref.shape[0]):
        weights = weights + jnp.where(lane == ids[:, k:k + 1], gains[:, k:k + 1], 0.0)
    table[me] = weights
    gated[...] = jnp.zeros_like(gated)
    upward[...] = jnp.zeros_like(upward)
    pl.semaphore_wait(barrier, N_DEV)

    tok_copy = remote(tok_ref, tok_sib, sem_tok.at[0], sem_tok.at[1], sibling)
    tok_copy.start()

    tok_copy.wait()
    for j in range(4):
        cols = slice(j * chunk, (j + 1) * chunk)
        mine, other = tok_ref[:, cols], tok_sib[:, cols]
        lower = jnp.where(c == 0, mine.astype(F32), other.astype(F32)).astype(BF16)
        upper = jnp.where(c == 0, other.astype(F32), mine.astype(F32)).astype(BF16)
        rows_x[x * 4 + j, row_at(z, y), :] = (
            jnp.concatenate([lower, upper], axis=0)
        )

    def spot(h, x_, z_, y_):
        return rows_x.at[
            x_ * 4 + c * 2 + h, row_at(z_, y_), :
        ]

    def label(h, x_, z_, y_):
        return h * 4 * NZ + x_ * N_PAIR + z_ * 2 + y_

    def along_line(h, z_, up):
        place = spot(h, x, z_, y)
        to = dev(x, z + 1 if up else z - 1, y, c)
        return remote(
            place, place, sem_line_s.at[h * 2 * NZ + (0 if up else NZ) + z_],
            sem_line_r.at[h * NZ + z_], to,
        )

    def first_hop(h, z_):
        place = spot(h, x, z_, y)
        return remote(
            place, place, sem_d1_s.at[h * NZ + z_], sem_d1_r.at[h * NZ + z_],
            y_peer if h == 0 else x_peer,
        )

    def first_arrived(h, z_):
        return (h, x, z_, 1 - y) if h == 0 else (h, 1 - x, z_, y)

    def first_wait(h, z_):
        place = spot(*first_arrived(h, z_))
        remote(place, place, sem_d1_s.at[h * NZ + z_], sem_d1_r.at[h * NZ + z_], sibling).wait_recv()

    def second_hop(h, z_, own):
        place = spot(h, x, z_, y) if own else spot(*first_arrived(h, z_))
        i = h * 2 * NZ + (0 if own else NZ) + z_
        return remote(
            place, place, sem_d2_s.at[i], sem_d2_r.at[i], x_peer if h == 0 else y_peer
        )

    def second_arrived(h, z_, own):
        if h == 0:
            return (h, 1 - x, z_, y if own else 1 - y)
        return (h, x if own else 1 - x, z_, 1 - y)

    def second_wait(h, z_, own):
        place = spot(*second_arrived(h, z_, own))
        i = h * 2 * NZ + (0 if own else NZ) + z_
        remote(place, place, sem_d2_s.at[i], sem_d2_r.at[i], sibling).wait_recv()

    def to_sibling(h, x_, z_, y_):
        place = spot(h, x_, z_, y_)
        i = label(h, x_, z_, y_)
        return remote(place, place, sem_core_s.at[i], sem_core_r.at[i], sibling)

    def from_sibling(h, x_, z_, y_):
        place = rows_x.at[
            x_ * 4 + (1 - c) * 2 + h, row_at(z_, y_), :
        ]
        i = label(h, x_, z_, y_)
        return remote(place, place, sem_core_s.at[i], sem_core_r.at[i], sibling)

    def level(k, fn):
        if k == 0:
            fn(z, None)
            return

        @pl.when(z - k >= 0)
        def _():
            fn(z - k, True)

        @pl.when(z + k < NZ)
        def _():
            fn(z + k, False)

    for h in range(2):
        @pl.when(z < NZ - 1)
        def _():
            along_line(h, z, True).start()

        @pl.when(z > 0)
        def _():
            along_line(h, z, False).start()

        first_hop(h, z).start()
        second_hop(h, z, True).start()

    for step in range(1, N_DEV):
        peer = (me + step) % N_DEV
        remote(
            table.at[me], table.at[me], sem_tab_s.at[step], sem_tab_r.at[me],
            {"section": x, "expert": peer},
        ).start()

    for k in range(1, NZ + 1):
        for h in range(2):
            if k < NZ:
                def arrived(z_, up):
                    place = spot(h, x, z_, y)
                    remote(
                        place, place, sem_line_s.at[h * 2 * NZ + z_], sem_line_r.at[h * NZ + z_],
                        sibling,
                    ).wait_recv()
                    if up:
                        @pl.when(z < NZ - 1)
                        def _():
                            along_line(h, z_, True).start()
                    else:
                        @pl.when(z > 0)
                        def _():
                            along_line(h, z_, False).start()
                    first_hop(h, z_).start()
                    second_hop(h, z_, True).start()
                    to_sibling(h, x, z_, y).start()

                level(k, arrived)
        for h in range(2):
            def arrived_first(z_, up):
                first_wait(h, z_)
                second_hop(h, z_, False).start()
                to_sibling(*first_arrived(h, z_)).start()

            level(k - 1, arrived_first)

    contract_last = (((1,), (1,)), ((), ()))
    weight_copies[0].wait()
    weight_copies[1].wait()
    half_rows = NZ * block

    def up_add(q, where):
        cols = pl.ds(pl.multiple_of(q * chunk, 128), chunk)
        inputs = rows_x[q, where, :]
        gated[where, :] += lax.dot_general(inputs, wg[:, cols], contract_last, preferred_element_type=F32)
        upward[where, :] += lax.dot_general(inputs, wu[:, cols], contract_last, preferred_element_type=F32)

    def up_all_rows(x_):
        def body(i, carry):
            up_add(x_ * 4 + i * 2, pl.ds(0, 2 * half_rows))
            return carry

        lax.fori_loop(0, 2, body, 0)

    def up_half_rows(y_):
        def body(i, carry):
            up_add(i * 2 + 1, pl.ds(pl.multiple_of(y_ * half_rows, half_rows), half_rows))
            return carry

        lax.fori_loop(0, 4, body, 0)

    def wait_sibling(h, x_, y_):
        for z_ in range(NZ):
            @pl.when(jnp.logical_or(x_ != x, jnp.logical_or(z_ != z, y_ != y)))
            def _():
                from_sibling(h, x_, z_, y_).wait_recv()

    def drain(items):
        for own, k in items:
            for h in range(2):
                def arrived_second(z_, up):
                    second_wait(h, z_, own)
                    to_sibling(*second_arrived(h, z_, own)).start()

                level(k, arrived_second)

    for y_ in (y, 1 - y):
        wait_sibling(0, x, y_)
    up_all_rows(x)
    drain(((True, 0), (True, 1), (False, 0), (True, 2)))
    for x_ in (x, 1 - x):
        wait_sibling(1, x_, y)
    up_half_rows(y)
    drain(((False, 1), (True, 3), (False, 2), (False, 3)))
    for y_ in (y, 1 - y):
        wait_sibling(0, 1 - x, y_)
    up_all_rows(1 - x)
    for x_ in (x, 1 - x):
        wait_sibling(1, x_, 1 - y)
    up_half_rows(1 - y)
    value = gated[...]
    hidden[...] = (value / (1.0 + jnp.exp(-value)) * upward[...]).astype(BF16)

    for step in range(1, N_DEV):
        peer = (me + N_DEV - step) % N_DEV
        remote(
            table.at[peer], table.at[peer], sem_tab_s.at[step], sem_tab_r.at[peer], sibling
        ).wait_recv()
    lane = lax.broadcasted_iota(jnp.int32, (N_DEV * count, 128), 1)
    every = jnp.concatenate([table[z_ * 4 + y_ * 2 + c_] for y_ in range(2) for z_ in range(NZ) for c_ in range(2)], axis=0)
    scale[...] = jnp.broadcast_to(
        jnp.sum(jnp.where(lane == me, every, 0.0), axis=1, keepdims=True), scale.shape
    )

    weight_copies[2].wait()
    n_rows = N_PAIR * block

    def down(x_, c_, h):
        q = x_ * 4 + c_ * 2 + h
        cols = pl.ds(pl.multiple_of(q * chunk, 128), chunk)
        return jnp.dot(hidden[...], wd[:, cols], preferred_element_type=F32) * scale[:, 0:1]

    def dest_at(j):
        a, b, d, e = ((3, 3, 0, 0), (2, 0, 3, 1), (1, 2, 1, 2), (0, 1, 2, 3))[j]
        return jnp.where(z == 0, a, jnp.where(z == 1, b, jnp.where(z == 2, d, e)))

    def core_copy(x_, h, z_, y_):
        i = x_ * 2 + h
        n = i * N_PAIR + z_ * 2 + y_
        return remote(
            core_out.at[i, row_at(z_, y_), :], core_in.at[i, row_at(z_, y_), :],
            sem_cx_s.at[n], sem_cx_r.at[n], sibling,
        )

    def order_step(i):
        return jnp.where(i < 2, 1 - x, x), jnp.where(jnp.logical_or(i == 1, i == 2), 1, 0)

    def send_step(i, carry):
        x_, h = order_step(i)
        core_out[x_ * 2 + h] = down(x_, 1 - c, h).astype(BF16)
        for j in range(NZ):
            for y_ in (1 - y, y):
                core_copy(x_, h, dest_at(j), y_).start()
        return carry

    lax.fori_loop(0, 4, send_step, 0)

    def keep_step(i, carry):
        x_, h = order_step(i)
        part[x_ * 2 + h] = down(x_, c, h)
        return carry

    lax.fori_loop(0, 4, keep_step, 0)

    def chip_sum(h, x_, z_, y_):
        i = x_ * 2 + h
        return part[i, row_at(z_, y_), :] + core_in[i, row_at(z_, y_), :].astype(F32)

    def first_slot(h, other, z_):
        return h * 2 * NZ + (NZ if other else 0) + z_

    def first_copy(h, other, z_):
        i = first_slot(h, other, z_)
        return remote(
            first_out.at[i], first_in.at[i], sem_f_s.at[i], sem_f_r.at[i],
            x_peer if h == 0 else y_peer,
        )

    def second_copy(h, z_):
        i = h * NZ + z_
        return remote(
            second_out.at[i], second_in.at[i], sem_s_s.at[i], sem_s_r.at[i],
            y_peer if h == 0 else x_peer,
        )

    zs = range(NZ)

    def first_send(z_):
        for other in (True, False):
            y_ = 1 - y if other else y
            core_copy(1 - x, 0, z_, y_).wait_recv()
            first_out[first_slot(0, other, z_)] = chip_sum(0, 1 - x, z_, y_).astype(BF16)
            first_copy(0, other, z_).start()
            x_ = 1 - x if other else x
            core_copy(x_, 1, z_, 1 - y).wait_recv()
            first_out[first_slot(1, other, z_)] = chip_sum(1, x_, z_, 1 - y).astype(BF16)
            first_copy(1, other, z_).start()

    def second_send(z_):
        for h in range(2):
            x_, y_ = (x, 1 - y) if h == 0 else (1 - x, y)
            core_copy(x_, h, z_, y_).wait_recv()
            first_copy(h, True, z_).wait_recv()
            second_out[h * NZ + z_] = (
                chip_sum(h, x_, z_, y_) + first_in[first_slot(h, True, z_)].astype(F32)
            ).astype(BF16)
            second_copy(h, z_).start()

    def gather_total(z_):
        for h in range(2):
            core_copy(x, h, z_, y).wait_recv()
            first_copy(h, False, z_).wait_recv()
            second_copy(h, z_).wait_recv()
            total[h * NZ + z_] = (
                chip_sum(h, x, z_, y)
                + first_in[first_slot(h, False, z_)].astype(F32)
                + second_in[h * NZ + z_].astype(F32)
            )

    def line_copy(h, up, dest):
        i = h * 2 * NZ + up * NZ + dest
        return remote(
            line_out.at[i], line_in.at[i], sem_l_s.at[i], sem_l_r.at[i],
            dev(x, jnp.where(up == 1, z + 1, z - 1), y, c),
        )

    def line_send(j, relayed):
        dest = dest_at(j)
        up = jnp.where(dest > z, 1, 0)
        feeds = jnp.where(up == 1, z, NZ - 1 - z) > 0

        @pl.when(feeds if relayed else jnp.logical_not(feeds))
        def _():
            for h in range(2):
                i = h * 2 * NZ + up * NZ + dest
                if relayed:
                    line_copy(h, up, dest).wait_recv()
                    line_out[i] = (total[h * NZ + dest] + line_in[i].astype(F32)).astype(BF16)
                else:
                    line_out[i] = total[h * NZ + dest].astype(BF16)
                line_copy(h, up, dest).start()

    for turn in range(NZ + 3):
        if turn < NZ:
            first_send(dest_at(turn))
        if 0 <= turn - 1 < NZ:
            second_send(dest_at(turn - 1))
        if 0 <= turn - 2 < NZ:
            gather_total(dest_at(turn - 2))
        if 0 <= turn - 2 < NZ - 1:
            line_send(turn - 2, False)
        if 0 <= turn - 3 < NZ - 1:
            line_send(turn - 3, True)

    for h in range(2):
        for up in range(2):
            @pl.when((z > 0) if up == 1 else (z < NZ - 1))
            def _():
                line_copy(h, up, z).wait_recv()
                total[h * NZ + z] += line_in[h * 2 * NZ + up * NZ + z].astype(F32)

    fin_copy = remote(fin_out, fin_in, sem_fin.at[0], sem_fin.at[1], sibling)
    halves = []
    for h in range(2):
        whole = total[h * NZ + z]
        lower, upper = whole[:count], whole[count:]
        fin_out[h] = jnp.where(c == 0, upper, lower).astype(BF16)
        halves.append(jnp.where(c == 0, lower, upper).astype(BF16))
    fin_copy.start()
    fin_copy.wait()
    for h in range(2):
        theirs = fin_in[h].astype(F32)
        mine = halves[h].astype(F32)
        out_ref[:, h * chunk:(h + 1) * chunk] = jnp.where(c == 0, mine, theirs).astype(BF16)
        out_ref[:, (2 + h) * chunk:(3 + h) * chunk] = jnp.where(c == 0, theirs, mine).astype(BF16)

    for step in range(1, N_DEV):
        remote(
            table.at[me], table.at[me], sem_tab_s.at[step], sem_tab_r.at[me], sibling
        ).wait_send()
    for h in range(2):
        for k in range(NZ):
            def sent(z_, up):
                if up is None or up:
                    @pl.when(z < NZ - 1)
                    def _():
                        along_line(h, z_, True).wait_send()
                if not up:
                    @pl.when(z > 0)
                    def _():
                        along_line(h, z_, False).wait_send()

            level(k, sent)
        for z_ in zs:
            first_hop(h, z_).wait_send()
            second_hop(h, z_, True).wait_send()
            second_hop(h, z_, False).wait_send()
            for x_ in range(2):
                for y_ in range(2):
                    @pl.when(jnp.logical_or(x_ != x, jnp.logical_or(z_ != z, y_ != y)))
                    def _():
                        to_sibling(h, x_, z_, y_).wait_send()
            first_copy(h, True, z_).wait_send()
            first_copy(h, False, z_).wait_send()
            second_copy(h, z_).wait_send()
        for x_ in range(2):
            for z_ in zs:
                for y_ in range(2):
                    core_copy(x_, h, z_, y_).wait_send()
    for j in range(NZ - 1):
        dest = dest_at(j)
        for h in range(2):
            line_copy(h, jnp.where(dest > z, 1, 0), dest).wait_send()


def fused(tokens, expert_ids, gate_weights, w_gate, w_up, w_down):
    count, share = tokens.shape
    hid, width = w_gate.shape[1:]
    chunk = share // 4
    block = 2 * count
    n_rows = N_PAIR * block
    dma = pltpu.SemaphoreType.DMA
    vmem = lambda shape, dtype: pltpu.VMEM(shape, dtype)
    blocks = lambda n: pltpu.VMEM((n, block, chunk), BF16)
    return pl.pallas_call(
        moe_kernel,
        out_shape=jax.ShapeDtypeStruct((count, share), BF16),
        in_specs=[pl.BlockSpec(memory_space=pltpu.VMEM)] * 3 + [pl.BlockSpec(memory_space=pl.ANY)] * 3,
        out_specs=pl.BlockSpec(memory_space=pltpu.VMEM),
        scratch_shapes=[
            vmem((hid, width), BF16), vmem((hid, width), BF16), vmem((hid, width), BF16),
            vmem((8, n_rows, chunk), BF16), vmem((count, share), BF16),
            vmem((N_DEV, count, 128), F32),
            vmem((n_rows, hid), F32), vmem((n_rows, hid), F32), vmem((n_rows, hid), BF16),
            vmem((n_rows, 128), F32),
            vmem((4, n_rows, chunk), F32), vmem((4, n_rows, chunk), BF16), vmem((4, n_rows, chunk), BF16),
            blocks(4 * NZ), blocks(4 * NZ), blocks(2 * NZ), blocks(2 * NZ),
            vmem((2 * NZ, block, chunk), F32), blocks(4 * NZ), blocks(4 * NZ),
            vmem((2, count, chunk), BF16), vmem((2, count, chunk), BF16),
            dma((3,)), dma((2,)), dma((N_DEV,)), dma((N_DEV,)),
            dma((4 * NZ,)), dma((2 * NZ,)), dma((2 * NZ,)), dma((2 * NZ,)),
            dma((4 * NZ,)), dma((4 * NZ,)), dma((8 * NZ,)), dma((8 * NZ,)),
            dma((8 * NZ,)), dma((8 * NZ,)), dma((4 * NZ,)), dma((4 * NZ,)), dma((2 * NZ,)), dma((2 * NZ,)),
            dma((4 * NZ,)), dma((4 * NZ,)), dma((2,)),
        ],
        compiler_params=pltpu.CompilerParams(
            collective_id=0, has_side_effects=True, vmem_limit_bytes=60 * 1024 * 1024
        ),
        cost_estimate=pl.CostEstimate(
            flops=6 * n_rows * hid * width, bytes_accessed=6 * hid * width,
            transcendentals=n_rows * hid,
        ),
    )(tokens, expert_ids.T, gate_weights.T, w_gate, w_up, w_down)


def on_device(tokens, expert_ids, gate_weights, w_gate, w_up, w_down):
    n_dest = lax.axis_size("expert")
    token_count = tokens.shape[0]
    chosen = expert_ids.shape[1]
    width = w_gate.shape[2]
    capacity = min(token_count, token_count * chosen * 4 // (3 * n_dest))
    flat_ids = expert_ids.reshape(-1)
    onehot = (flat_ids[:, None] == jnp.arange(n_dest, dtype=jnp.int32)[None, :]).astype(jnp.int32)
    order_rank = jnp.cumsum(onehot, axis=0) - 1
    slot_index = jnp.sum(order_rank * onehot, axis=1)
    target = flat_ids * capacity + slot_index
    token_of = jnp.arange(token_count * chosen, dtype=jnp.int32) // chosen
    matches = (jnp.arange(n_dest * capacity, dtype=jnp.int32)[:, None] == target[None, :]).astype(
        jnp.bfloat16
    )
    token_map = (token_of[:, None] == jnp.arange(token_count, dtype=jnp.int32)[None, :]).astype(
        jnp.bfloat16
    )
    dispatch_matrix = jnp.dot(matches, token_map, preferred_element_type=jnp.float32).astype(
        jnp.bfloat16
    )
    scaled_map = token_map * gate_weights.reshape(-1)[:, None]
    combine_matrix = jnp.dot(scaled_map.T, matches.T, preferred_element_type=jnp.float32).astype(
        jnp.bfloat16
    )
    contract_last = (((1,), (1,)), ((), ()))
    features = lax.all_gather(tokens, "section", axis=1, tiled=True)
    send_rows = jnp.dot(dispatch_matrix, features, preferred_element_type=jnp.float32).astype(
        jnp.bfloat16
    )
    send_rows = send_rows.reshape(n_dest, capacity, width)
    received = lax.all_to_all(send_rows, "expert", split_axis=0, concat_axis=0, tiled=True)
    inputs = received.reshape(-1, width)
    gated = lax.dot_general(inputs, w_gate[0], contract_last, preferred_element_type=jnp.float32)
    upward = lax.dot_general(inputs, w_up[0], contract_last, preferred_element_type=jnp.float32)
    hidden = (jax.nn.silu(gated) * upward).astype(jnp.bfloat16)
    partial_value = jnp.dot(hidden, w_down[0], preferred_element_type=jnp.float32).astype(
        jnp.bfloat16
    )
    partial_value = partial_value.reshape((received.shape[0], received.shape[1], width))
    returned = lax.all_to_all(partial_value, "expert", split_axis=0, concat_axis=0, tiled=True)
    weighted = jnp.dot(
        combine_matrix, returned.reshape(-1, width), preferred_element_type=jnp.float32
    )
    return lax.psum_scatter(weighted, "section", scatter_dimension=1, tiled=True).astype(
        jnp.bfloat16
    )


def solution(mesh):
    placed = (
        P("expert", "section"),
        P("expert", None),
        P("expert", None),
        P("expert", "section", None),
        P("expert", "section", None),
        P("expert", "section", None),
    )
    whole_kernel = mesh.shape["section"] == 2 and mesh.shape["expert"] == N_DEV
    return jax.shard_map(
        fused if whole_kernel else on_device, mesh=mesh, in_specs=placed, out_specs=P("expert", "section"), check_vma=False
    )
```
